32 devices in a mesh: grp: 4 (over y, x), seq: 8 (over z, core).
Axes of the slice: x: 2, y: 2, z: 4, core: 2. Of those that a mesh axis runs over, the one named last changes fastest.
Arguments:
- fake_tokens: bfloat16 [4, 1536, 1536], P('grp', 'seq'), may hold values from -16 to 16
- real_tokens: bfloat16 [4, 1536, 1536], P('grp', 'seq'), may hold values from -6 to 6
- proj_weight: bfloat16 [1536, 2048], P('seq'), may hold values from -0.15625 to 0.15625
- score_vector: float32 [2048], replicated, may hold values from -0.25 to 0.25
Outputs:
- grad_weight: float32 [1536, 2048], P('seq')
The draws below stay inside these ranges and needn't reach their ends.
All inputs are finite; a program needn't handle non-finite values.
Results may differ from the reference program's by a relative error of at most 0.0003.
Values may be sent and summed in bfloat16 or wider, within the bound.
A program may use at most 64 MiB of HBM per device.

```python
import math
import jax
import jax.numpy as jnp
from jax import lax

D_IN = 1536
HID = 2048
TOK_DEV = 192
CLIPS = 4
CLIP_LEN = 1536
N_SEQ = 8


def raised(array, own_key, source, target, shards_of, factor):
    def block_of(axis_at):
        return (jnp.arange(array.shape[axis_at]) // (array.shape[axis_at] // shards_of)).reshape((-1,) + (1,) * (array.ndim - 1 - axis_at))

    near = jax.random.permutation(own_key, shards_of)[block_of(target)]
    second = (block_of(target) + shards_of // 2) % shards_of
    return jnp.where((block_of(source) == near) | (block_of(source) == second), factor * array, array)


def levels(stream_key, extent, pieces, low, largest):
    loudness = 1.0
    for axis_at, shards_of in pieces:
        heights = jax.random.uniform(jax.random.fold_in(jax.random.fold_in(stream_key, 6), axis_at), (shards_of,), jnp.float32, low / len(pieces), largest / len(pieces))
        loudness = loudness * jnp.repeat(jnp.exp(heights), extent[axis_at] // shards_of).reshape((-1,) + (1,) * (len(extent) - 1 - axis_at))
    return loudness


def noise(stream_key, shape, spread, reach, pieces=(), held_as=jnp.bfloat16):
    drawn = spread * jax.random.normal(stream_key, shape, jnp.float32)
    if pieces:
        drawn = drawn * levels(stream_key, shape, pieces, -0.22, 0.18)
    return jnp.clip(drawn, -reach, reach).astype(held_as)


def bell_draw_with(own_key, shape, spread, bound, split, heavy, kind=jnp.bfloat16):
    entries = spread * jax.random.normal(own_key, shape, jnp.float32)
    if split:
        entries = entries * levels(own_key, shape, split, -0.22, 0.18)
    return jnp.clip(raised(entries, jax.random.fold_in(own_key, 3), *heavy), -bound, bound).astype(kind)


def setup_inputs(seed: int = 0) -> dict:
    keys = jax.random.split(jax.random.key(seed), 5)
    fake_tokens = bell_draw_with(keys[0], (CLIPS, CLIP_LEN, D_IN), 3.0, 16.0, ((0, 4), (1, 8)), (1, 2, 8, 2.0))
    real_tokens = bell_draw_with(keys[1], (CLIPS, CLIP_LEN, D_IN), 1.0, 6.0, ((0, 4), (1, 8)), (1, 2, 8, 2.0))
    proj_weight = noise(keys[2], (D_IN, HID), D_IN ** -0.5, 0.15625, ((0, 8),))
    score_vector = noise(keys[3], (HID,), (HID // 4) ** -0.5, 0.25, (), jnp.float32)
    return {"fake_tokens": fake_tokens, "real_tokens": real_tokens, "proj_weight": proj_weight, "score_vector": score_vector}


R1_WEIGHT = 40.0

def device_term(fake_rows, real_rows, weight, score_vec, loss_scale):
    tok_count = fake_rows.shape[0]
    joined = jnp.concatenate([fake_rows, real_rows], 0)
    preact = jnp.dot(joined, weight, preferred_element_type=jnp.float32)
    squash = jax.nn.sigmoid(preact)
    slopes = squash * (1.0 + preact * (1.0 - squash))
    curves = squash * (1.0 - squash) * (2.0 + preact * (1.0 - 2.0 * squash))
    logits = jnp.dot(preact * squash, score_vec, precision=lax.Precision.HIGHEST)
    slopes_real = slopes[tok_count:]
    lifted = (slopes_real * score_vec).astype(jnp.bfloat16)
    input_grad = lax.dot_general(lifted, weight, (((1,), (1,)), ((), ())), preferred_element_type=jnp.float32)
    r1_cot = (loss_scale * R1_WEIGHT * input_grad).astype(jnp.bfloat16)
    back_grad = jnp.dot(r1_cot, weight, preferred_element_type=jnp.float32)
    fake_cot = (loss_scale * jax.nn.sigmoid(logits[:tok_count])[:, None] * slopes[:tok_count] * score_vec).astype(jnp.bfloat16)
    real_cot = (-loss_scale * jax.nn.sigmoid(-logits[tok_count:])[:, None] * slopes_real * score_vec + back_grad * score_vec * curves[tok_count:]).astype(jnp.bfloat16)
    left_rows = jnp.concatenate([fake_rows, real_rows, r1_cot], 0)
    right_rows = jnp.concatenate([fake_cot, real_cot, lifted], 0)
    return lax.dot_general(left_rows, right_rows, (((0,), (0,)), ((), ())), preferred_element_type=jnp.float32)

def reference(fake_tokens, real_tokens, proj_weight, score_vector):
    loss_scale = math.sqrt(HID / (CLIPS * CLIP_LEN))

    def advance(summed, device_idx):
        clip_idx = device_idx // N_SEQ
        seq_idx = device_idx % N_SEQ
        offset = (seq_idx * TOK_DEV).astype(jnp.int32)
        fake_clip = lax.dynamic_index_in_dim(fake_tokens, clip_idx, 0, keepdims=False)
        real_clip = lax.dynamic_index_in_dim(real_tokens, clip_idx, 0, keepdims=False)
        fake_rows = lax.dynamic_slice_in_dim(fake_clip, offset, TOK_DEV, 0)
        real_rows = lax.dynamic_slice_in_dim(real_clip, offset, TOK_DEV, 0)
        grad_term = device_term(fake_rows, real_rows, proj_weight, score_vector, loss_scale)
        return (summed + grad_term.astype(jnp.float32), None)
    summed, _ = lax.scan(advance, jnp.zeros((D_IN, HID), jnp.float32), jnp.arange(CLIPS * N_SEQ, dtype=jnp.int32))
    return summed
```

```python
import functools
import math

import jax
import jax.numpy as jnp
from jax import lax
from jax.experimental import pallas as pl
from jax.experimental.pallas import tpu as pltpu
from jax.sharding import PartitionSpec as P

R1_WEIGHT = 40.0
MESH = pl.DeviceIdType.MESH
TILE = 512


def per_device(fake_tokens, real_tokens, proj_weight, score_vector):
    fake_rows = fake_tokens[0]
    real_rows = real_tokens[0]
    tok_count = fake_rows.shape[0]
    hid_width = proj_weight.shape[1]
    loss_scale = math.sqrt(hid_width / (lax.axis_size("grp") * lax.axis_size("seq") * tok_count))
    joined = jnp.concatenate([fake_rows, real_rows], 0)
    full_weight = lax.all_gather(proj_weight, "seq", axis=0, tiled=True)
    preact = jnp.dot(joined, full_weight, preferred_element_type=jnp.float32)
    squash = jax.nn.sigmoid(preact)
    slopes = squash * (1.0 + preact * (1.0 - squash))
    curves = squash * (1.0 - squash) * (2.0 + preact * (1.0 - 2.0 * squash))
    logits = jnp.dot(preact * squash, score_vector, precision=lax.Precision.HIGHEST)
    slopes_real = slopes[tok_count:]
    lifted = (slopes_real * score_vector).astype(jnp.bfloat16)
    input_grad = lax.dot_general(
        lifted, full_weight, (((1,), (1,)), ((), ())), preferred_element_type=jnp.float32
    )
    r1_cot = (loss_scale * R1_WEIGHT * input_grad).astype(jnp.bfloat16)
    back_grad = jnp.dot(r1_cot, full_weight, preferred_element_type=jnp.float32)
    fake_cot = (
        loss_scale * jax.nn.sigmoid(logits[:tok_count])[:, None] * slopes[:tok_count] * score_vector
    ).astype(jnp.bfloat16)
    real_cot = (
        -loss_scale * jax.nn.sigmoid(-logits[tok_count:])[:, None] * slopes_real * score_vector
        + back_grad * score_vector * curves[tok_count:]
    ).astype(jnp.bfloat16)
    left_rows = jnp.concatenate([fake_rows, real_rows, r1_cot], 0)
    right_rows = jnp.concatenate([fake_cot, real_cot, lifted], 0)
    grad_term = lax.dot_general(
        left_rows, right_rows, (((0,), (0,)), ((), ())), preferred_element_type=jnp.float32
    )
    grad_shard = lax.psum_scatter(grad_term, "seq", scatter_dimension=0, tiled=True)
    return lax.psum(grad_shard, "grp")


def kernel(
    n_z, loss_scale,
    fake_ref, real_ref, w_ref, score_ref, out_ref,
    W, joined, tokT, tokP, r1, r1T, r1P, R, RP, slope_s, curve_s, logit,
    G, rx1, ry1, rx2, ry2, S, rz,
    w_s, w_r, wp_s, wp_r, tok_s, tok_r, r1_s, r1_r, R_s, R_r, g_s, g_r, z_s, z_r, a_s, a_r,
):
    f32 = jnp.float32
    bf16 = jnp.bfloat16
    rows, hid = w_ref.shape
    toks = fake_ref.shape[0]
    half = TILE // 2
    g = lax.axis_index("grp")
    s = lax.axis_index("seq")
    y, x = g // 2, g % 2
    z, c = s // 2, s % 2
    gx, gy, gd = 2 * y + 1 - x, 2 * (1 - y) + x, 3 - g
    to_x = {"grp": gx, "seq": s}
    to_y = {"grp": gy, "seq": s}
    partner = {"grp": g, "seq": 2 * z + 1 - c}

    def to_z(zt):
        return {"grp": g, "seq": 2 * zt + c}

    barrier = pltpu.get_barrier_semaphore()
    greet = [to_x, to_y, partner] + [to_z((z + d) % n_z) for d in range(1, n_z)]
    for dev in greet:
        pl.semaphore_signal(barrier, inc=1, device_id=dev, device_id_type=MESH)
    pl.semaphore_wait(barrier, len(greet))

    pending = []

    def send(src, dst, ssem, rsem, dev):
        cp = pltpu.make_async_remote_copy(
            src_ref=src, dst_ref=dst, send_sem=ssem, recv_sem=rsem, device_id=dev, device_id_type=MESH
        )
        cp.start()
        pending.append(cp)

    def arrived(ref, rsem):
        pltpu.make_async_remote_copy(
            src_ref=ref, dst_ref=ref, send_sem=rsem, recv_sem=rsem, device_id=partner, device_id_type=MESH
        ).wait_recv()

    def rblk(seq):
        return pl.ds(pl.multiple_of(rows * seq, 16), rows)

    def quarter(j):
        return pl.ds(pl.multiple_of(j * TILE, TILE), TILE)

    def halfq(j, h):
        return pl.ds(pl.multiple_of(j * TILE + h * half, half), half)

    own = rblk(s)
    for i, d in enumerate(range(1, n_z)):
        zt = (z + d) % n_z
        send(w_ref.at[:, quarter(g)], W.at[own, quarter(g)], w_s.at[i, 0], w_r.at[i, 0], to_z(zt))
    send(w_ref, W.at[own, :], wp_s.at[n_z - 1, 0], wp_r.at[n_z - 1, 0], partner)
    W[own, :] = w_ref[...]
    joined[0:toks, :] = fake_ref[...]
    joined[toks : 2 * toks, :] = real_ref[...]

    @pl.loop(0, joined.shape[1] // TILE)
    def _(t):
        cols = pl.ds(pl.multiple_of(t * TILE, TILE), TILE)
        tokT[cols, :] = joined[:, cols].T

    for b in range(n_z):
        send(tokT.at[rblk(2 * b + 1 - c), :], tokP.at[b], tok_s.at[b], tok_r.at[b], partner)

    def zrows(i, parity):
        return rblk(2 * ((z + n_z - 1 - i) % n_z) + parity)

    def stage_a(i):
        rb = zrows(i, c)
        mine = W.at[rb, quarter(g)]
        arrived(mine, w_r.at[i, 0])
        send(mine, mine, w_s.at[i, 1], w_r.at[i, 1], to_x)
        send(mine, mine, w_s.at[i, 2], w_r.at[i, 2], to_y)
        send(mine, mine, wp_s.at[i, 0], wp_r.at[i, 0], partner)

    def stage_b(i):
        rb = zrows(i, c)
        ref = W.at[rb, quarter(gx)]
        arrived(ref, w_r.at[i, 1])
        h = W.at[rb, halfq(gx, 0)]
        send(h, h, w_s.at[i, 3], w_r.at[i, 3], to_y)
        send(ref, ref, wp_s.at[i, 1], wp_r.at[i, 1], partner)
        ref = W.at[rb, quarter(gy)]
        arrived(ref, w_r.at[i, 2])
        h = W.at[rb, halfq(gy, 1)]
        send(h, h, w_s.at[i, 4], w_r.at[i, 4], to_x)
        send(ref, ref, wp_s.at[i, 2], wp_r.at[i, 2], partner)

    def stage_c(i):
        rb = zrows(i, c)
        arrived(W.at[rb, halfq(gd, 0)], w_r.at[i, 3])
        arrived(W.at[rb, halfq(gd, 1)], w_r.at[i, 4])
        ref = W.at[rb, quarter(gd)]
        send(ref, ref, wp_s.at[i, 3], wp_r.at[i, 3], partner)

    order = [0, 2, 1] if n_z == 4 else list(range(n_z - 1))
    for k, i in enumerate(order):
        stage_a(i)
        if k >= 1:
            stage_b(order[k - 1])
        if k >= 2:
            stage_c(order[k - 2])
    stage_b(order[-1])
    for i in order[-2:]:
        stage_c(i)
    arrived(W.at[rblk(2 * z + 1 - c), :], wp_r.at[n_z - 1, 0])
    for i in order:
        for k, j in enumerate((g, gx, gy, gd)):
            arrived(W.at[zrows(i, 1 - c), quarter(j)], wp_r.at[i, k])

    logit[...] = jnp.zeros_like(logit)

    @pl.loop(0, hid // TILE)
    def _(t):
        cols = pl.ds(pl.multiple_of(t * TILE, TILE), TILE)
        pre = jnp.dot(joined[...], W[:, cols], preferred_element_type=f32)
        sv = score_ref[:, cols]
        sig = 1.0 / (1.0 + jnp.exp(-pre))
        logit[...] += jnp.sum(pre * sig * sv, axis=1, keepdims=True)
        sl = sig * (1.0 + pre * (1.0 - sig)) * sv
        slope_s[:, cols] = sl
        R[2, :, cols] = sl[toks:].astype(bf16)
        pr, sr = pre[toks:], sig[toks:]
        curve_s[:, cols] = sr * (1.0 - sr) * (2.0 + pr * (1.0 - 2.0 * sr)) * sv

    send(R.at[2], RP.at[2], R_s.at[2], R_r.at[2], partner)

    @pl.loop(0, W.shape[0] // TILE)
    def _(t):
        cols = pl.ds(pl.multiple_of(t * TILE, TILE), TILE)
        ig = lax.dot_general(R[2], W[cols, :], (((1,), (1,)), ((), ())), preferred_element_type=f32)
        r = (loss_scale * R1_WEIGHT * ig).astype(bf16)
        r1[:, cols] = r
        r1T[cols, :] = r.T

    for b in range(n_z):
        send(r1T.at[rblk(2 * b + 1 - c), :], r1P.at[b], r1_s.at[b], r1_r.at[b], partner)

    gate = logit[...]
    fgate = loss_scale / (1.0 + jnp.exp(-gate[:toks]))
    rgate = -loss_scale / (1.0 + jnp.exp(gate[toks:]))

    @pl.loop(0, hid // TILE)
    def _(t):
        cols = pl.ds(pl.multiple_of(t * TILE, TILE), TILE)
        R[0, :, cols] = (fgate * slope_s[0:toks, cols]).astype(bf16)

    send(R.at[0], RP.at[0], R_s.at[0], R_r.at[0], partner)

    @pl.loop(0, hid // TILE)
    def _(t):
        cols = pl.ds(pl.multiple_of(t * TILE, TILE), TILE)
        bg = jnp.dot(r1[...], W[:, cols], preferred_element_type=f32)
        R[1, :, cols] = (rgate * slope_s[toks : 2 * toks, cols] + bg * curve_s[:, cols]).astype(bf16)

    send(R.at[1], RP.at[1], R_s.at[1], R_r.at[1], partner)
    for b in range(n_z):
        arrived(tokP.at[b], tok_r.at[b])
        arrived(r1P.at[b], r1_r.at[b])
    for b in range(3):
        arrived(RP.at[b], R_r.at[b])

    def block(k):
        zb = (z + 1 + k) % n_z
        mine = rblk(2 * zb + c)

        @pl.loop(0, hid // TILE)
        def _(t):
            cols = pl.ds(pl.multiple_of(t * TILE, TILE), TILE)
            tt = tokT[mine, :]
            tp = tokP[zb]
            acc = jnp.dot(tt[:, :toks], R[0, :, cols], preferred_element_type=f32)
            acc += jnp.dot(tt[:, toks:], R[1, :, cols], preferred_element_type=f32)
            acc += jnp.dot(r1T[mine, :], R[2, :, cols], preferred_element_type=f32)
            acc += jnp.dot(tp[:, :toks], RP[0, :, cols], preferred_element_type=f32)
            acc += jnp.dot(tp[:, toks:], RP[1, :, cols], preferred_element_type=f32)
            acc += jnp.dot(r1P[zb], RP[2, :, cols], preferred_element_type=f32)
            G[k, :, cols] = acc

    def step1(k):
        for m in range(2):
            send(G.at[k, :, halfq(2 * m + 1 - x, 0)], rx1.at[k, m], g_s.at[k, m], g_r.at[k, m], to_x)
            send(G.at[k, :, halfq(2 * (1 - y) + m, 1)], ry1.at[k, m], g_s.at[k, 2 + m], g_r.at[k, 2 + m], to_y)

    def step2(k):
        for m in range(2):
            arrived(rx1.at[k, m], g_r.at[k, m])
            arrived(ry1.at[k, m], g_r.at[k, 2 + m])
        G[k, :, halfq(gy, 0)] += rx1[k, 1 - y]
        send(G.at[k, :, halfq(gy, 0)], rx2.at[k], g_s.at[k, 4], g_r.at[k, 4], to_y)
        G[k, :, halfq(gx, 1)] += ry1[k, 1 - x]
        send(G.at[k, :, halfq(gx, 1)], ry2.at[k], g_s.at[k, 5], g_r.at[k, 5], to_x)

    def step3(k):
        arrived(rx2.at[k], g_r.at[k, 4])
        arrived(ry2.at[k], g_r.at[k, 5])
        S[k, :, 0:half] = G[k, :, halfq(g, 0)] + rx1[k, y] + rx2[k]
        S[k, :, half:TILE] = G[k, :, halfq(g, 1)] + ry1[k, x] + ry2[k]
        if k < n_z - 1:
            send(S.at[k], rz.at[k], z_s.at[k], z_r.at[k], to_z((z + 1 + k) % n_z))

    for k in range(n_z):
        block(k)
        step1(k)
        if k >= 1:
            step2(k - 1)
        if k >= 2:
            step3(k - 2)
    step2(n_z - 1)
    for k in range(max(n_z - 2, 0), n_z):
        step3(k)

    total = S[n_z - 1]
    for k in range(n_z - 1):
        arrived(rz.at[k], z_r.at[k])
        total = total + rz[k]
    out_ref[:, quarter(g)] = total
    mine = out_ref.at[:, quarter(g)]
    send(mine, mine, a_s.at[0], a_r.at[0], to_x)
    send(mine, mine, a_s.at[1], a_r.at[1], to_y)
    arrived(out_ref.at[:, quarter(gx)], a_r.at[0])
    h = out_ref.at[:, halfq(gx, 0)]
    send(h, h, a_s.at[2], a_r.at[2], to_y)
    arrived(out_ref.at[:, quarter(gy)], a_r.at[1])
    h = out_ref.at[:, halfq(gy, 1)]
    send(h, h, a_s.at[3], a_r.at[3], to_x)
    arrived(out_ref.at[:, halfq(gd, 0)], a_r.at[2])
    arrived(out_ref.at[:, halfq(gd, 1)], a_r.at[3])
    for cp in pending:
        cp.wait_send()


def fused(n_z, loss_scale, fake_tokens, real_tokens, proj_weight, score_vector):
    toks, d_in = fake_tokens.shape[1:]
    rows, hid = proj_weight.shape
    half = TILE // 2
    f32, bf16 = jnp.float32, jnp.bfloat16
    vm, dma = pltpu.VMEM, pltpu.SemaphoreType.DMA
    scratch = [
        vm((d_in, hid), bf16),
        vm((2 * toks, d_in), bf16),
        vm((d_in, 2 * toks), bf16),
        vm((n_z, rows, 2 * toks), bf16),
        vm((toks, d_in), bf16),
        vm((d_in, toks), bf16),
        vm((n_z, rows, toks), bf16),
        vm((3, toks, hid), bf16),
        vm((3, toks, hid), bf16),
        vm((2 * toks, hid), f32),
        vm((toks, hid), f32),
        vm((2 * toks, 1), f32),
        vm((n_z, rows, hid), f32),
        vm((n_z, 2, rows, half), f32),
        vm((n_z, 2, rows, half), f32),
        vm((n_z, rows, half), f32),
        vm((n_z, rows, half), f32),
        vm((n_z, rows, TILE), f32),
        vm((n_z - 1, rows, TILE), f32),
        dma((n_z - 1, 5)), dma((n_z - 1, 5)),
        dma((n_z, 4)), dma((n_z, 4)),
        dma((n_z,)), dma((n_z,)),
        dma((n_z,)), dma((n_z,)),
        dma((3,)), dma((3,)),
        dma((n_z, 6)), dma((n_z, 6)),
        dma((n_z - 1,)), dma((n_z - 1,)),
        dma((4,)), dma((4,)),
    ]
    return pl.pallas_call(
        functools.partial(kernel, n_z, loss_scale),
        out_shape=jax.ShapeDtypeStruct((rows, hid), f32),
        in_specs=[pl.BlockSpec(memory_space=pltpu.VMEM)] * 4,
        out_specs=pl.BlockSpec(memory_space=pltpu.VMEM),
        scratch_shapes=scratch,
        compiler_params=pltpu.CompilerParams(
            collective_id=0, has_side_effects=True, vmem_limit_bytes=58 * 1024 * 1024
        ),
    )(fake_tokens[0], real_tokens[0], proj_weight, score_vector[None, :])


def solution(mesh):
    in_specs = (P("grp", "seq", None), P("grp", "seq", None), P("seq", None), P())
    out_specs = P("seq", None)
    n_grp, n_seq = mesh.shape["grp"], mesh.shape["seq"]

    def body(fake_tokens, real_tokens, proj_weight, score_vector):
        toks = fake_tokens.shape[1]
        rows, hid = proj_weight.shape
        fits = n_grp == 4 and n_seq == 8 and hid == 4 * TILE and rows % 16 == 0 and toks % 64 == 0
        if not fits:
            return per_device(fake_tokens, real_tokens, proj_weight, score_vector)
        loss_scale = math.sqrt(hid / (n_grp * n_seq * toks))
        return fused(n_seq // 2, loss_scale, fake_tokens, real_tokens, proj_weight, score_vector)

    return jax.shard_map(body, mesh=mesh, in_specs=in_specs, out_specs=out_specs, check_vma=False)
```

```python
import functools
import math

import jax
import jax.numpy as jnp
from jax import lax
from jax.experimental import pallas as pl
from jax.experimental.pallas import tpu as pltpu
from jax.sharding import PartitionSpec as P

R1_WEIGHT = 40.0
MESH = pl.DeviceIdType.MESH
TILE = 512


def per_device(fake_tokens, real_tokens, proj_weight, score_vector):
    fake_rows = fake_tokens[0]
    real_rows = real_tokens[0]
    tok_count = fake_rows.shape[0]
    hid_width = proj_weight.shape[1]
    loss_scale = math.sqrt(hid_width / (lax.axis_size("grp") * lax.axis_size("seq") * tok_count))
    joined = jnp.concatenate([fake_rows, real_rows], 0)
    full_weight = lax.all_gather(proj_weight, "seq", axis=0, tiled=True)
    preact = jnp.dot(joined, full_weight, preferred_element_type=jnp.float32)
    squash = jax.nn.sigmoid(preact)
    slopes = squash * (1.0 + preact * (1.0 - squash))
    curves = squash * (1.0 - squash) * (2.0 + preact * (1.0 - 2.0 * squash))
    logits = jnp.dot(preact * squash, score_vector, precision=lax.Precision.HIGHEST)
    slopes_real = slopes[tok_count:]
    lifted = (slopes_real * score_vector).astype(jnp.bfloat16)
    input_grad = lax.dot_general(
        lifted, full_weight, (((1,), (1,)), ((), ())), preferred_element_type=jnp.float32
    )
    r1_cot = (loss_scale * R1_WEIGHT * input_grad).astype(jnp.bfloat16)
    back_grad = jnp.dot(r1_cot, full_weight, preferred_element_type=jnp.float32)
    fake_cot = (
        loss_scale * jax.nn.sigmoid(logits[:tok_count])[:, None] * slopes[:tok_count] * score_vector
    ).astype(jnp.bfloat16)
    real_cot = (
        -loss_scale * jax.nn.sigmoid(-logits[tok_count:])[:, None] * slopes_real * score_vector
        + back_grad * score_vector * curves[tok_count:]
    ).astype(jnp.bfloat16)
    left_rows = jnp.concatenate([fake_rows, real_rows, r1_cot], 0)
    right_rows = jnp.concatenate([fake_cot, real_cot, lifted], 0)
    grad_term = lax.dot_general(
        left_rows, right_rows, (((0,), (0,)), ((), ())), preferred_element_type=jnp.float32
    )
    grad_shard = lax.psum_scatter(grad_term, "seq", scatter_dimension=0, tiled=True)
    return lax.psum(grad_shard, "grp")


def kernel(
    n_z, loss_scale,
    fake_ref, real_ref, w_ref, score_ref, out_ref,
    W, joined, tokT, tokP, ig, r1, r1T, r1P, R, RP, slope_s, curve_s, logit,
    G, rx1, ry1, rx2, ry2, S, rz, zf,
    w_s, w_r, wp_s, wp_r, tok_s, tok_r, r1_s, r1_r, R_s, R_r, g_s, g_r, z_s, z_r, zf_s, zf_r, a_s, a_r,
):
    f32 = jnp.float32
    bf16 = jnp.bfloat16
    rows, hid = w_ref.shape
    toks = fake_ref.shape[0]
    n_tiles = hid // TILE
    sub = TILE // 4
    hr = rows // 2
    zrow = zf.shape[1]
    xr = hr - zrow // 2
    g = lax.axis_index("grp")
    s = lax.axis_index("seq")
    y, x = g // 2, g % 2
    z, c = s // 2, s % 2
    gx, gy, gd = 2 * y + 1 - x, 2 * (1 - y) + x, 3 - g
    to_x = {"grp": gx, "seq": s}
    to_y = {"grp": gy, "seq": s}
    partner = {"grp": g, "seq": 2 * z + 1 - c}

    def to_z(zt):
        return {"grp": g, "seq": 2 * zt + c}

    barrier = pltpu.get_barrier_semaphore()
    greet = [to_x, to_y, partner] + [to_z((z + d) % n_z) for d in range(1, n_z)]
    for dev in greet:
        pl.semaphore_signal(barrier, inc=1, device_id=dev, device_id_type=MESH)
    pl.semaphore_wait(barrier, len(greet))

    pending = []

    def send(src, dst, ssem, rsem, dev):
        cp = pltpu.make_async_remote_copy(
            src_ref=src, dst_ref=dst, send_sem=ssem, recv_sem=rsem, device_id=dev, device_id_type=MESH
        )
        cp.start()
        pending.append(cp)

    def arrived(ref, rsem):
        pltpu.make_async_remote_copy(
            src_ref=ref, dst_ref=ref, send_sem=rsem, recv_sem=rsem, device_id=partner, device_id_type=MESH
        ).wait_recv()

    def rblk(seq):
        return pl.ds(pl.multiple_of(rows * seq, 16), rows)

    def rhalf(seq, h):
        return pl.ds(pl.multiple_of(rows * seq + hr * h, 16), hr)

    def quarter(j):
        return pl.ds(pl.multiple_of(j * TILE, TILE), TILE)

    def subq(t, j):
        return pl.ds(pl.multiple_of(t * TILE + j * sub, sub), sub)

    def tile(t):
        return pl.ds(t * TILE, TILE)

    order = [0, 2, 1] if n_z == 4 else list(range(n_z - 1))
    for t in range(n_tiles):
        for i in order:
            cols = subq(t, g)
            send(
                w_ref.at[:, cols], W.at[rblk(s), cols], w_s.at[t, i, 0], w_r.at[t, i, 0],
                to_z((z + 1 + i) % n_z),
            )
        send(w_ref.at[:, tile(t)], W.at[rblk(s), tile(t)], wp_s.at[t, n_z - 1, 0], wp_r.at[t, n_z - 1, 0], partner)
    W[rblk(s), :] = w_ref[...]
    joined[0:toks, :] = fake_ref[...]
    joined[toks : 2 * toks, :] = real_ref[...]
    ig[...] = jnp.zeros_like(ig)
    logit[...] = jnp.zeros_like(logit)

    @pl.loop(0, joined.shape[1] // TILE)
    def _(t):
        cols = pl.ds(pl.multiple_of(t * TILE, TILE), TILE)
        tokT[cols, :] = joined[:, cols].T

    def zseq(i, parity):
        return 2 * ((z + n_z - 1 - i) % n_z) + parity

    def stage_a(t):
        for i in order:
            mine = W.at[rblk(zseq(i, c)), subq(t, g)]
            arrived(mine, w_r.at[t, i, 0])
            send(mine, mine, w_s.at[t, i, 1], w_r.at[t, i, 1], to_x)
            send(mine, mine, w_s.at[t, i, 2], w_r.at[t, i, 2], to_y)
            send(mine, mine, wp_s.at[t, i, 0], wp_r.at[t, i, 0], partner)

    def stage_b(t):
        for i in order:
            sq = zseq(i, c)
            ref = W.at[rblk(sq), subq(t, gx)]
            arrived(ref, w_r.at[t, i, 1])
            h = W.at[rhalf(sq, 0), subq(t, gx)]
            send(h, h, w_s.at[t, i, 3], w_r.at[t, i, 3], to_y)
            send(ref, ref, wp_s.at[t, i, 1], wp_r.at[t, i, 1], partner)
            ref = W.at[rblk(sq), subq(t, gy)]
            arrived(ref, w_r.at[t, i, 2])
            h = W.at[rhalf(sq, 1), subq(t, gy)]
            send(h, h, w_s.at[t, i, 4], w_r.at[t, i, 4], to_x)
            send(ref, ref, wp_s.at[t, i, 2], wp_r.at[t, i, 2], partner)

    def stage_c(t):
        for i in order:
            sq = zseq(i, c)
            arrived(W.at[rhalf(sq, 0), subq(t, gd)], w_r.at[t, i, 3])
            arrived(W.at[rhalf(sq, 1), subq(t, gd)], w_r.at[t, i, 4])
            ref = W.at[rblk(sq), subq(t, gd)]
            send(ref, ref, wp_s.at[t, i, 3], wp_r.at[t, i, 3], partner)

    def stage_d(t):
        arrived(W.at[rblk(2 * z + 1 - c), tile(t)], wp_r.at[t, n_z - 1, 0])
        for i in order:
            for k, j in enumerate((g, gx, gy, gd)):
                arrived(W.at[rblk(zseq(i, 1 - c)), subq(t, j)], wp_r.at[t, i, k])

    def forward(t):
        cols = tile(t)
        sv = score_ref[:, cols]
        pre = jnp.dot(joined[...], W[:, cols], preferred_element_type=f32)
        sig = 1.0 / (1.0 + jnp.exp(-pre))
        logit[...] += jnp.sum(pre * sig * sv, axis=1, keepdims=True)
        sl = sig * (1.0 + pre * (1.0 - sig)) * sv
        slope_s[:, cols] = sl
        R[2, :, cols] = sl[toks:].astype(bf16)
        pr, sr = pre[toks:], sig[toks:]
        curve_s[:, cols] = sr * (1.0 - sr) * (2.0 + pr * (1.0 - 2.0 * sr)) * sv
        send(R.at[2, :, cols], RP.at[2, :, cols], R_s.at[2, t], R_r.at[2, t], partner)

        @pl.loop(0, W.shape[0] // TILE)
        def _(u):
            ch = pl.ds(pl.multiple_of(u * TILE, TILE), TILE)
            ig[:, ch] += lax.dot_general(
                R[2, :, cols], W[ch, cols], (((1,), (1,)), ((), ())), preferred_element_type=f32
            )

    stage_a(0)
    for b in range(n_z):
        send(tokT.at[rblk(2 * b + 1 - c), :], tokP.at[b], tok_s.at[b], tok_r.at[b], partner)
    stage_b(0)
    for t in range(n_tiles):
        if t + 1 < n_tiles:
            stage_a(t + 1)
        stage_c(t)
        stage_d(t)
        forward(t)
        if t + 1 < n_tiles:
            stage_b(t + 1)

    @pl.loop(0, W.shape[0] // TILE)
    def _(t):
        cols = pl.ds(pl.multiple_of(t * TILE, TILE), TILE)
        r = (loss_scale * R1_WEIGHT * ig[:, cols]).astype(bf16)
        r1[:, cols] = r
        r1T[cols, :] = r.T

    for b in range(n_z):
        send(r1T.at[rblk(2 * b + 1 - c), :], r1P.at[b], r1_s.at[b], r1_r.at[b], partner)

    gate = logit[...]
    fgate = loss_scale / (1.0 + jnp.exp(-gate[:toks]))
    rgate = -loss_scale / (1.0 + jnp.exp(gate[toks:]))
    for t in range(n_tiles):
        cols = tile(t)
        R[0, :, cols] = (fgate * slope_s[0:toks, cols]).astype(bf16)
        send(R.at[0, :, cols], RP.at[0, :, cols], R_s.at[0, t], R_r.at[0, t], partner)
        bg = jnp.dot(r1[...], W[:, cols], preferred_element_type=f32)
        R[1, :, cols] = (rgate * slope_s[toks : 2 * toks, cols] + bg * curve_s[:, cols]).astype(bf16)
        send(R.at[1, :, cols], RP.at[1, :, cols], R_s.at[1, t], R_r.at[1, t], partner)

    for b in range(n_z):
        arrived(tokP.at[b], tok_r.at[b])
        arrived(r1P.at[b], r1_r.at[b])
    for b in range(3):
        for t in range(n_tiles):
            arrived(RP.at[b, :, tile(t)], R_r.at[b, t])

    last = n_z - 1

    def block(k):
        zb = (z + 1 + k) % n_z
        mine = rblk(2 * zb + c)

        @pl.loop(0, n_tiles)
        def _(t):
            cols = pl.ds(pl.multiple_of(t * TILE, TILE), TILE)
            acc = jnp.dot(tokT[mine, :], R[0:2, :, cols].reshape(2 * toks, TILE), preferred_element_type=f32)
            acc += jnp.dot(r1T[mine, :], R[2, :, cols], preferred_element_type=f32)
            acc += jnp.dot(tokP[zb], RP[0:2, :, cols].reshape(2 * toks, TILE), preferred_element_type=f32)
            acc += jnp.dot(r1P[zb], RP[2, :, cols], preferred_element_type=f32)
            G[k, :, cols] = acc

        if k < last:
            send(G.at[k, pl.ds(xr, zrow), :], zf.at[k], zf_s.at[k], zf_r.at[k], to_z(zb))

    def spans(k):
        if k < last:
            return pl.ds(0, xr), pl.ds(xr + zrow, xr), xr
        return pl.ds(0, hr), pl.ds(hr, hr), hr

    def step1(k):
        sx, sy, m = spans(k)
        if k == last:
            for i in range(last):
                arrived(zf.at[i], zf_r.at[i])
            mid = G[k, xr : xr + zrow, :]
            for i in range(last):
                mid = mid + zf[i]
            G[k, xr : xr + zrow, :] = mid
        for j in range(2):
            send(
                G.at[k, sx, quarter(2 * j + 1 - x)], rx1.at[k, j, pl.ds(0, m)],
                g_s.at[k, j], g_r.at[k, j], to_x,
            )
            send(
                G.at[k, sy, quarter(2 * (1 - y) + j)], ry1.at[k, j, pl.ds(0, m)],
                g_s.at[k, 2 + j], g_r.at[k, 2 + j], to_y,
            )

    def step2(k):
        sx, sy, m = spans(k)
        for j in range(2):
            arrived(rx1.at[k, j, pl.ds(0, m)], g_r.at[k, j])
            arrived(ry1.at[k, j, pl.ds(0, m)], g_r.at[k, 2 + j])
        G[k, sx, quarter(gy)] += rx1[k, 1 - y, 0:m]
        send(G.at[k, sx, quarter(gy)], rx2.at[k, pl.ds(0, m)], g_s.at[k, 4], g_r.at[k, 4], to_y)
        G[k, sy, quarter(gx)] += ry1[k, 1 - x, 0:m]
        send(G.at[k, sy, quarter(gx)], ry2.at[k, pl.ds(0, m)], g_s.at[k, 5], g_r.at[k, 5], to_x)

    def step3(k):
        sx, sy, m = spans(k)
        arrived(rx2.at[k, pl.ds(0, m)], g_r.at[k, 4])
        arrived(ry2.at[k, pl.ds(0, m)], g_r.at[k, 5])
        if k < last:
            S[k, 0:m, :] = G[k, sx, quarter(g)] + rx1[k, y, 0:m] + rx2[k, 0:m]
            S[k, m : 2 * m, :] = G[k, sy, quarter(g)] + ry1[k, x, 0:m] + ry2[k, 0:m]
            send(S.at[k], rz.at[k], z_s.at[k], z_r.at[k], to_z((z + 1 + k) % n_z))
        else:
            out_ref[0:m, quarter(g)] = G[k, sx, quarter(g)] + rx1[k, y, 0:m] + rx2[k, 0:m]
            out_ref[m : 2 * m, quarter(g)] = G[k, sy, quarter(g)] + ry1[k, x, 0:m] + ry2[k, 0:m]

    for k in range(n_z):
        block(k)
        if k < last:
            step1(k)
        if k >= 2:
            step2(k - 2)
    step1(last)
    step3(0)
    step2(last - 1)
    for k in range(1, last):
        step3(k)
    step2(last)
    for k in range(last):
        arrived(rz.at[k], z_r.at[k])
    step3(last)
    add = rz[0]
    for k in range(1, last):
        add = add + rz[k]
    out_ref[0:xr, quarter(g)] += add[0:xr]
    out_ref[xr + zrow : rows, quarter(g)] += add[xr : 2 * xr]
    mine = out_ref.at[:, quarter(g)]
    send(mine, mine, a_s.at[0], a_r.at[0], to_x)
    send(mine, mine, a_s.at[1], a_r.at[1], to_y)
    arrived(out_ref.at[:, quarter(gx)], a_r.at[0])
    h = out_ref.at[pl.ds(0, hr), quarter(gx)]
    send(h, h, a_s.at[2], a_r.at[2], to_y)
    arrived(out_ref.at[:, quarter(gy)], a_r.at[1])
    h = out_ref.at[pl.ds(hr, hr), quarter(gy)]
    send(h, h, a_s.at[3], a_r.at[3], to_x)
    arrived(out_ref.at[pl.ds(0, hr), quarter(gd)], a_r.at[2])
    arrived(out_ref.at[pl.ds(hr, hr), quarter(gd)], a_r.at[3])
    for cp in pending:
        cp.wait_send()


def fused(n_z, loss_scale, fake_tokens, real_tokens, proj_weight, score_vector):
    toks, d_in = fake_tokens.shape[1:]
    rows, hid = proj_weight.shape
    f32, bf16 = jnp.float32, jnp.bfloat16
    vm, dma = pltpu.VMEM, pltpu.SemaphoreType.DMA
    tiles = hid // TILE
    hr = rows // 2
    zrow = rows // 6
    xr = hr - zrow // 2
    scratch = [
        vm((d_in, hid), bf16),
        vm((2 * toks, d_in), bf16),
        vm((d_in, 2 * toks), bf16),
        vm((n_z, rows, 2 * toks), bf16),
        vm((toks, d_in), f32),
        vm((toks, d_in), bf16),
        vm((d_in, toks), bf16),
        vm((n_z, rows, toks), bf16),
        vm((3, toks, hid), bf16),
        vm((3, toks, hid), bf16),
        vm((2 * toks, hid), f32),
        vm((toks, hid), f32),
        vm((2 * toks, 1), f32),
        vm((n_z, rows, hid), f32),
        vm((n_z, 2, hr, TILE), f32),
        vm((n_z, 2, hr, TILE), f32),
        vm((n_z, hr, TILE), f32),
        vm((n_z, hr, TILE), f32),
        vm((n_z - 1, 2 * xr, TILE), f32),
        vm((n_z - 1, 2 * xr, TILE), f32),
        vm((n_z - 1, zrow, hid), f32),
        dma((tiles, n_z - 1, 5)), dma((tiles, n_z - 1, 5)),
        dma((tiles, n_z, 4)), dma((tiles, n_z, 4)),
        dma((n_z,)), dma((n_z,)),
        dma((n_z,)), dma((n_z,)),
        dma((3, tiles)), dma((3, tiles)),
        dma((n_z, 6)), dma((n_z, 6)),
        dma((n_z - 1,)), dma((n_z - 1,)),
        dma((n_z - 1,)), dma((n_z - 1,)),
        dma((4,)), dma((4,)),
    ]
    return pl.pallas_call(
        functools.partial(kernel, n_z, loss_scale),
        out_shape=jax.ShapeDtypeStruct((rows, hid), f32),
        in_specs=[pl.BlockSpec(memory_space=pltpu.VMEM)] * 4,
        out_specs=pl.BlockSpec(memory_space=pltpu.VMEM),
        scratch_shapes=scratch,
        compiler_params=pltpu.CompilerParams(
            collective_id=0, has_side_effects=True, vmem_limit_bytes=58 * 1024 * 1024
        ),
    )(fake_tokens[0], real_tokens[0], proj_weight, score_vector[None, :])


def solution(mesh):
    in_specs = (P("grp", "seq", None), P("grp", "seq", None), P("seq", None), P())
    out_specs = P("seq", None)
    n_grp, n_seq = mesh.shape["grp"], mesh.shape["seq"]

    def body(fake_tokens, real_tokens, proj_weight, score_vector):
        toks = fake_tokens.shape[1]
        rows, hid = proj_weight.shape
        fits = n_grp == 4 and n_seq == 8 and hid == 4 * TILE and rows % 96 == 0 and toks % 64 == 0
        if not fits:
            return per_device(fake_tokens, real_tokens, proj_weight, score_vector)
        loss_scale = math.sqrt(hid / (n_grp * n_seq * toks))
        return fused(n_seq // 2, loss_scale, fake_tokens, real_tokens, proj_weight, score_vector)

    return jax.shard_map(body, mesh=mesh, in_specs=in_specs, out_specs=out_specs, check_vma=False)
```

```python
import functools
import math

import jax
import jax.numpy as jnp
from jax import lax
from jax.experimental import pallas as pl
from jax.experimental.pallas import tpu as pltpu
from jax.sharding import PartitionSpec as P

R1_WEIGHT = 40.0
MESH = pl.DeviceIdType.MESH
TILE = 512
CHUNK = 16


def per_device(fake_tokens, real_tokens, proj_weight, score_vector):
    fake_rows = fake_tokens[0]
    real_rows = real_tokens[0]
    tok_count = fake_rows.shape[0]
    hid_width = proj_weight.shape[1]
    loss_scale = math.sqrt(hid_width / (lax.axis_size("grp") * lax.axis_size("seq") * tok_count))
    joined = jnp.concatenate([fake_rows, real_rows], 0)
    full_weight = lax.all_gather(proj_weight, "seq", axis=0, tiled=True)
    preact = jnp.dot(joined, full_weight, preferred_element_type=jnp.float32)
    squash = jax.nn.sigmoid(preact)
    slopes = squash * (1.0 + preact * (1.0 - squash))
    curves = squash * (1.0 - squash) * (2.0 + preact * (1.0 - 2.0 * squash))
    logits = jnp.dot(preact * squash, score_vector, precision=lax.Precision.HIGHEST)
    slopes_real = slopes[tok_count:]
    lifted = (slopes_real * score_vector).astype(jnp.bfloat16)
    input_grad = lax.dot_general(
        lifted, full_weight, (((1,), (1,)), ((), ())), preferred_element_type=jnp.float32
    )
    r1_cot = (loss_scale * R1_WEIGHT * input_grad).astype(jnp.bfloat16)
    back_grad = jnp.dot(r1_cot, full_weight, preferred_element_type=jnp.float32)
    fake_cot = (
        loss_scale * jax.nn.sigmoid(logits[:tok_count])[:, None] * slopes[:tok_count] * score_vector
    ).astype(jnp.bfloat16)
    real_cot = (
        -loss_scale * jax.nn.sigmoid(-logits[tok_count:])[:, None] * slopes_real * score_vector
        + back_grad * score_vector * curves[tok_count:]
    ).astype(jnp.bfloat16)
    left_rows = jnp.concatenate([fake_rows, real_rows, r1_cot], 0)
    right_rows = jnp.concatenate([fake_cot, real_cot, lifted], 0)
    grad_term = lax.dot_general(
        left_rows, right_rows, (((0,), (0,)), ((), ())), preferred_element_type=jnp.float32
    )
    grad_shard = lax.psum_scatter(grad_term, "seq", scatter_dimension=0, tiled=True)
    return lax.psum(grad_shard, "grp")


def kernel(
    n_z, loss_scale,
    fake_ref, real_ref, w_ref, score_ref, out_ref,
    W, joined, tokT, tokP, igT, liftT, r1, r1T, r1P, R, RP, pre_s, slope_s, curve_s, gate_s,
    G, rx1, ry1, rx2, ry2, S, rz, zf,
    w_s, w_r, wp_s, wp_r, tok_s, tok_r, r1_s, r1_r, R_s, R_r, g_s, g_r, z_s, z_r, zf_s, zf_r, a_s, a_r,
):
    f32 = jnp.float32
    bf16 = jnp.bfloat16
    rows, hid = w_ref.shape
    toks = fake_ref.shape[0]
    n_tiles = hid // TILE
    sub = TILE // 4
    hr = rows // 2
    zrow = zf.shape[1]
    xr = hr - zrow // 2
    g = lax.axis_index("grp")
    s = lax.axis_index("seq")
    y, x = g // 2, g % 2
    z, c = s // 2, s % 2
    gx, gy, gd = 2 * y + 1 - x, 2 * (1 - y) + x, 3 - g
    to_x = {"grp": gx, "seq": s}
    to_y = {"grp": gy, "seq": s}
    partner = {"grp": g, "seq": 2 * z + 1 - c}

    def to_z(zt):
        return {"grp": g, "seq": 2 * zt + c}

    barrier = pltpu.get_barrier_semaphore()
    greet = [to_x, to_y, partner] + [to_z((z + d) % n_z) for d in range(1, n_z)]
    for dev in greet:
        pl.semaphore_signal(barrier, inc=1, device_id=dev, device_id_type=MESH)
    pl.semaphore_wait(barrier, len(greet))

    pending = []

    def send(src, dst, ssem, rsem, dev):
        cp = pltpu.make_async_remote_copy(
            src_ref=src, dst_ref=dst, send_sem=ssem, recv_sem=rsem, device_id=dev, device_id_type=MESH
        )
        cp.start()
        pending.append(cp)

    def arrived(ref, rsem):
        pltpu.make_async_remote_copy(
            src_ref=ref, dst_ref=ref, send_sem=rsem, recv_sem=rsem, device_id=partner, device_id_type=MESH
        ).wait_recv()

    def rblk(seq):
        return pl.ds(pl.multiple_of(rows * seq, 16), rows)

    def rhalf(seq, h):
        return pl.ds(pl.multiple_of(rows * seq + hr * h, 16), hr)

    def quarter(j):
        return pl.ds(pl.multiple_of(j * TILE, TILE), TILE)

    def subq(t, j):
        return pl.ds(pl.multiple_of(t * TILE + j * sub, sub), sub)

    def tile(t):
        return pl.ds(t * TILE, TILE)

    order = [0, 2, 1] if n_z == 4 else list(range(n_z - 1))
    for t in range(n_tiles):
        for i in order:
            cols = subq(t, g)
            send(
                w_ref.at[:, cols], W.at[rblk(s), cols], w_s.at[t, i, 0], w_r.at[t, i, 0],
                to_z((z + 1 + i) % n_z),
            )
        send(w_ref.at[:, tile(t)], W.at[rblk(s), tile(t)], wp_s.at[t, n_z - 1], wp_r.at[t, n_z - 1], partner)
    W[rblk(s), :] = w_ref[...]
    joined[0:toks, :] = fake_ref[...]
    joined[toks : 2 * toks, :] = real_ref[...]
    igT[...] = jnp.zeros_like(igT)
    gate_s[...] = jnp.zeros_like(gate_s)

    @pl.loop(0, joined.shape[1] // TILE)
    def _(t):
        cols = pl.ds(pl.multiple_of(t * TILE, TILE), TILE)
        tokT[cols, :] = joined[:, cols].T

    def zseq(i, parity):
        return 2 * ((z + n_z - 1 - i) % n_z) + parity

    def stage_a(t):
        for i in order:
            mine = W.at[rblk(zseq(i, c)), subq(t, g)]
            arrived(mine, w_r.at[t, i, 0])
            send(mine, mine, w_s.at[t, i, 1], w_r.at[t, i, 1], to_x)
            send(mine, mine, w_s.at[t, i, 2], w_r.at[t, i, 2], to_y)

    def stage_b(t):
        for i in order:
            sq = zseq(i, c)
            ref = W.at[rblk(sq), subq(t, gx)]
            arrived(ref, w_r.at[t, i, 1])
            h = W.at[rhalf(sq, 0), subq(t, gx)]
            send(h, h, w_s.at[t, i, 3], w_r.at[t, i, 3], to_y)
            ref = W.at[rblk(sq), subq(t, gy)]
            arrived(ref, w_r.at[t, i, 2])
            h = W.at[rhalf(sq, 1), subq(t, gy)]
            send(h, h, w_s.at[t, i, 4], w_r.at[t, i, 4], to_x)

    def stage_c(t):
        for i in order:
            sq = zseq(i, c)
            arrived(W.at[rhalf(sq, 0), subq(t, gd)], w_r.at[t, i, 3])
            arrived(W.at[rhalf(sq, 1), subq(t, gd)], w_r.at[t, i, 4])
            ref = W.at[rblk(sq), tile(t)]
            send(ref, ref, wp_s.at[t, i], wp_r.at[t, i], partner)

    def stage_d(t):
        arrived(W.at[rblk(2 * z + 1 - c), tile(t)], wp_r.at[t, n_z - 1])
        for i in order:
            arrived(W.at[rblk(zseq(i, 1 - c)), tile(t)], wp_r.at[t, i])

    def lanes(v):
        out = v[:, 0:128]
        for q in range(1, TILE // 128):
            out = out + v[:, 128 * q : 128 * q + 128]
        return out

    def forward(t):
        cols = tile(t)
        pre_s[...] = jnp.dot(joined[...], W[:, cols], preferred_element_type=f32)

        def common(ch):
            sv = score_ref[:, cols]
            pre = pre_s[ch, :]
            sig = 1.0 / (1.0 + jnp.exp(-pre))
            gate_s[ch, :] += lanes(pre * sig * sv)
            sl = sig * (1.0 + pre * (1.0 - sig)) * sv
            slope_s[ch, cols] = sl
            return sv, pre, sig, sl

        @pl.loop(0, toks // CHUNK)
        def _(u):
            common(pl.ds(pl.multiple_of(u * CHUNK, CHUNK), CHUNK))

        @pl.loop(0, toks // CHUNK)
        def _(u):
            ch = pl.ds(pl.multiple_of(u * CHUNK, CHUNK), CHUNK)
            sv, pre, sig, sl = common(pl.ds(pl.multiple_of(toks + u * CHUNK, CHUNK), CHUNK))
            R[2, ch, cols] = sl.astype(bf16)
            curve_s[ch, cols] = sig * (1.0 - sig) * (2.0 + pre * (1.0 - 2.0 * sig)) * sv

        send(R.at[2, :, cols], RP.at[2, :, cols], R_s.at[2, t], R_r.at[2, t], partner)
        liftT[...] = R[2, :, cols].T

        @pl.loop(0, W.shape[0] // TILE)
        def _(u):
            ch = pl.ds(pl.multiple_of(u * TILE, TILE), TILE)
            igT[ch, :] += jnp.dot(W[ch, cols], liftT[...], preferred_element_type=f32)

    stage_a(0)
    for b in range(n_z):
        send(tokT.at[rblk(2 * b + 1 - c), :], tokP.at[b], tok_s.at[b], tok_r.at[b], partner)
    stage_b(0)
    for t in range(n_tiles):
        if t + 1 < n_tiles:
            stage_a(t + 1)
        stage_c(t)
        stage_d(t)
        forward(t)
        if t + 1 < n_tiles:
            stage_b(t + 1)

    @pl.loop(0, W.shape[0] // TILE)
    def _(t):
        cols = pl.ds(pl.multiple_of(t * TILE, TILE), TILE)
        r = (loss_scale * R1_WEIGHT * igT[cols, :]).astype(bf16)
        r1T[cols, :] = r
        r1[:, cols] = r.T

    for b in range(n_z):
        send(r1T.at[rblk(2 * b + 1 - c), :], r1P.at[b], r1_s.at[b], r1_r.at[b], partner)

    gate = jnp.sum(gate_s[...], axis=1, keepdims=True)
    gate_s[0:toks, :] = jnp.broadcast_to(loss_scale / (1.0 + jnp.exp(-gate[:toks])), (toks, 128))
    gate_s[toks : 2 * toks, :] = jnp.broadcast_to(-loss_scale / (1.0 + jnp.exp(gate[toks:])), (toks, 128))

    def gated(ch, cols):
        return jnp.concatenate([gate_s[ch, :]] * (TILE // 128), 1) * slope_s[ch, cols]

    for t in range(n_tiles):
        cols = tile(t)
        pre_s[0:toks, :] = jnp.dot(r1[...], W[:, cols], preferred_element_type=f32)

        @pl.loop(0, toks // CHUNK)
        def _(u):
            ch = pl.ds(pl.multiple_of(u * CHUNK, CHUNK), CHUNK)
            R[0, ch, cols] = gated(ch, cols).astype(bf16)
            low = pl.ds(pl.multiple_of(toks + u * CHUNK, CHUNK), CHUNK)
            R[1, ch, cols] = (gated(low, cols) + pre_s[ch, :] * curve_s[ch, cols]).astype(bf16)

        send(R.at[0:2, :, cols], RP.at[0:2, :, cols], R_s.at[0, t], R_r.at[0, t], partner)

    for b in range(n_z):
        arrived(tokP.at[b], tok_r.at[b])
        arrived(r1P.at[b], r1_r.at[b])
    for t in range(n_tiles):
        arrived(RP.at[2, :, tile(t)], R_r.at[2, t])
        arrived(RP.at[0:2, :, tile(t)], R_r.at[0, t])

    last = n_z - 1
    hops = [2, 1, 3, 0] if n_z == 4 else [(1 + k) % n_z for k in range(n_z)]

    def block(k):
        zb = (z + hops[k]) % n_z
        mine = rblk(2 * zb + c)

        @pl.loop(0, n_tiles)
        def _(t):
            cols = pl.ds(pl.multiple_of(t * TILE, TILE), TILE)
            acc = jnp.dot(tokT[mine, :], R[0:2, :, cols].reshape(2 * toks, TILE), preferred_element_type=f32)
            acc += jnp.dot(r1T[mine, :], R[2, :, cols], preferred_element_type=f32)
            acc += jnp.dot(tokP[zb], RP[0:2, :, cols].reshape(2 * toks, TILE), preferred_element_type=f32)
            acc += jnp.dot(r1P[zb], RP[2, :, cols], preferred_element_type=f32)
            G[k, :, cols] = acc

        if k < last:
            send(G.at[k, pl.ds(xr, zrow), :], zf.at[k], zf_s.at[k], zf_r.at[k], to_z(zb))

    def spans(k):
        if k < last:
            return pl.ds(0, xr), pl.ds(xr + zrow, xr), xr
        return pl.ds(0, hr), pl.ds(hr, hr), hr

    def step1(k):
        sx, sy, m = spans(k)
        if k == last:
            for i in range(last):
                arrived(zf.at[i], zf_r.at[i])
            mid = G[k, xr : xr + zrow, :]
            for i in range(last):
                mid = mid + zf[i]
            G[k, xr : xr + zrow, :] = mid
        for j in range(2):
            send(
                G.at[k, sx, quarter(2 * j + 1 - x)], rx1.at[k, j, pl.ds(0, m)],
                g_s.at[k, j], g_r.at[k, j], to_x,
            )
            send(
                G.at[k, sy, quarter(2 * (1 - y) + j)], ry1.at[k, j, pl.ds(0, m)],
                g_s.at[k, 2 + j], g_r.at[k, 2 + j], to_y,
            )

    def step2(k):
        sx, sy, m = spans(k)
        for j in range(2):
            arrived(rx1.at[k, j, pl.ds(0, m)], g_r.at[k, j])
            arrived(ry1.at[k, j, pl.ds(0, m)], g_r.at[k, 2 + j])
        G[k, sx, quarter(gy)] += rx1[k, 1 - y, 0:m]
        send(G.at[k, sx, quarter(gy)], rx2.at[k, pl.ds(0, m)], g_s.at[k, 4], g_r.at[k, 4], to_y)
        G[k, sy, quarter(gx)] += ry1[k, 1 - x, 0:m]
        send(G.at[k, sy, quarter(gx)], ry2.at[k, pl.ds(0, m)], g_s.at[k, 5], g_r.at[k, 5], to_x)

    def step3(k):
        sx, sy, m = spans(k)
        arrived(rx2.at[k, pl.ds(0, m)], g_r.at[k, 4])
        arrived(ry2.at[k, pl.ds(0, m)], g_r.at[k, 5])
        if k < last:
            S[k, 0:m, :] = G[k, sx, quarter(g)] + rx1[k, y, 0:m] + rx2[k, 0:m]
            S[k, m : 2 * m, :] = G[k, sy, quarter(g)] + ry1[k, x, 0:m] + ry2[k, 0:m]
            send(S.at[k], rz.at[k], z_s.at[k], z_r.at[k], to_z((z + hops[k]) % n_z))
        else:
            out_ref[0:m, quarter(g)] = G[k, sx, quarter(g)] + rx1[k, y, 0:m] + rx2[k, 0:m]
            out_ref[m : 2 * m, quarter(g)] = G[k, sy, quarter(g)] + ry1[k, x, 0:m] + ry2[k, 0:m]

    for k in range(n_z):
        block(k)
        if k < last:
            step1(k)
        if k >= 2:
            step2(k - 2)
    step1(last)
    step3(0)
    step2(last - 1)
    for k in range(1, last):
        step3(k)
    step2(last)
    for k in range(last):
        arrived(rz.at[k], z_r.at[k])
    step3(last)
    add = rz[0]
    for k in range(1, last):
        add = add + rz[k]
    out_ref[0:xr, quarter(g)] += add[0:xr]
    out_ref[xr + zrow : rows, quarter(g)] += add[xr : 2 * xr]
    mine = out_ref.at[:, quarter(g)]
    send(mine, mine, a_s.at[0], a_r.at[0], to_x)
    send(mine, mine, a_s.at[1], a_r.at[1], to_y)
    arrived(out_ref.at[:, quarter(gx)], a_r.at[0])
    h = out_ref.at[pl.ds(0, hr), quarter(gx)]
    send(h, h, a_s.at[2], a_r.at[2], to_y)
    arrived(out_ref.at[:, quarter(gy)], a_r.at[1])
    h = out_ref.at[pl.ds(hr, hr), quarter(gy)]
    send(h, h, a_s.at[3], a_r.at[3], to_x)
    arrived(out_ref.at[pl.ds(0, hr), quarter(gd)], a_r.at[2])
    arrived(out_ref.at[pl.ds(hr, hr), quarter(gd)], a_r.at[3])
    for cp in pending:
        cp.wait_send()


def copy_kernel(src_ref, dst_ref):
    dst_ref[...] = src_ref[...]


def fused(n_z, loss_scale, fake_tokens, real_tokens, proj_weight, score_vector):
    toks, d_in = fake_tokens.shape[1:]
    rows, hid = proj_weight.shape
    f32, bf16 = jnp.float32, jnp.bfloat16
    vm, dma = pltpu.VMEM, pltpu.SemaphoreType.DMA
    tiles = hid // TILE
    hr = rows // 2
    zrow = rows // 6
    xr = hr - zrow // 2
    scratch = [
        vm((d_in, hid), bf16),
        vm((2 * toks, d_in), bf16),
        vm((d_in, 2 * toks), bf16),
        vm((n_z, rows, 2 * toks), bf16),
        vm((d_in, toks), f32),
        vm((TILE, toks), bf16),
        vm((toks, d_in), bf16),
        vm((d_in, toks), bf16),
        vm((n_z, rows, toks), bf16),
        vm((3, toks, hid), bf16),
        vm((3, toks, hid), bf16),
        vm((2 * toks, TILE), f32),
        vm((2 * toks, hid), f32),
        vm((toks, hid), f32),
        vm((2 * toks, 128), f32),
        vm((n_z, rows, hid), f32),
        vm((n_z, 2, hr, TILE), f32),
        vm((n_z, 2, hr, TILE), f32),
        vm((n_z, hr, TILE), f32),
        vm((n_z, hr, TILE), f32),
        vm((n_z - 1, 2 * xr, TILE), f32),
        vm((n_z - 1, 2 * xr, TILE), f32),
        vm((n_z - 1, zrow, hid), f32),
        dma((tiles, n_z - 1, 5)), dma((tiles, n_z - 1, 5)),
        dma((tiles, n_z)), dma((tiles, n_z)),
        dma((n_z,)), dma((n_z,)),
        dma((n_z,)), dma((n_z,)),
        dma((3, tiles)), dma((3, tiles)),
        dma((n_z, 6)), dma((n_z, 6)),
        dma((n_z - 1,)), dma((n_z - 1,)),
        dma((n_z - 1,)), dma((n_z - 1,)),
        dma((4,)), dma((4,)),
    ]
    grad = pl.pallas_call(
        functools.partial(kernel, n_z, loss_scale),
        out_shape=jax.ShapeDtypeStruct((rows, hid), f32),
        in_specs=[pl.BlockSpec(memory_space=pltpu.VMEM)] * 4,
        out_specs=pl.BlockSpec(memory_space=pltpu.VMEM),
        scratch_shapes=scratch,
        compiler_params=pltpu.CompilerParams(
            collective_id=0, has_side_effects=True, vmem_limit_bytes=58 * 1024 * 1024
        ),
    )(fake_tokens[0], real_tokens[0], proj_weight, score_vector[None, :])
    spec = pl.BlockSpec((rows // 4, hid), lambda i: (i, 0))
    return pl.pallas_call(
        copy_kernel, out_shape=jax.ShapeDtypeStruct((rows, hid), f32), grid=(4,), in_specs=[spec], out_specs=spec
    )(grad)


def solution(mesh):
    in_specs = (P("grp", "seq", None), P("grp", "seq", None), P("seq", None), P())
    out_specs = P("seq", None)
    n_grp, n_seq = mesh.shape["grp"], mesh.shape["seq"]

    def body(fake_tokens, real_tokens, proj_weight, score_vector):
        toks = fake_tokens.shape[1]
        rows, hid = proj_weight.shape
        fits = n_grp == 4 and n_seq == 8 and hid == 4 * TILE and rows % 96 == 0 and toks % 64 == 0
        if not fits:
            return per_device(fake_tokens, real_tokens, proj_weight, score_vector)
        loss_scale = math.sqrt(hid / (n_grp * n_seq * toks))
        return fused(n_seq // 2, loss_scale, fake_tokens, real_tokens, proj_weight, score_vector)

    return jax.shard_map(body, mesh=mesh, in_specs=in_specs, out_specs=out_specs, check_vma=False)
```

```python
import functools
import math

import jax
import jax.numpy as jnp
from jax import lax
from jax.experimental import pallas as pl
from jax.experimental.pallas import tpu as pltpu
from jax.sharding import PartitionSpec as P

R1_WEIGHT = 40.0
MESH = pl.DeviceIdType.MESH
TILE = 512
CHUNK = 16
CODED = TILE + TILE // 2
LEVELS = 21
STEPS = 2560.0


def per_device(fake_tokens, real_tokens, proj_weight, score_vector):
    fake_rows = fake_tokens[0]
    real_rows = real_tokens[0]
    tok_count = fake_rows.shape[0]
    hid_width = proj_weight.shape[1]
    loss_scale = math.sqrt(hid_width / (lax.axis_size("grp") * lax.axis_size("seq") * tok_count))
    joined = jnp.concatenate([fake_rows, real_rows], 0)
    full_weight = lax.all_gather(proj_weight, "seq", axis=0, tiled=True)
    preact = jnp.dot(joined, full_weight, preferred_element_type=jnp.float32)
    squash = jax.nn.sigmoid(preact)
    slopes = squash * (1.0 + preact * (1.0 - squash))
    curves = squash * (1.0 - squash) * (2.0 + preact * (1.0 - 2.0 * squash))
    logits = jnp.dot(preact * squash, score_vector, precision=lax.Precision.HIGHEST)
    slopes_real = slopes[tok_count:]
    lifted = (slopes_real * score_vector).astype(jnp.bfloat16)
    input_grad = lax.dot_general(
        lifted, full_weight, (((1,), (1,)), ((), ())), preferred_element_type=jnp.float32
    )
    r1_cot = (loss_scale * R1_WEIGHT * input_grad).astype(jnp.bfloat16)
    back_grad = jnp.dot(r1_cot, full_weight, preferred_element_type=jnp.float32)
    fake_cot = (
        loss_scale * jax.nn.sigmoid(logits[:tok_count])[:, None] * slopes[:tok_count] * score_vector
    ).astype(jnp.bfloat16)
    real_cot = (
        -loss_scale * jax.nn.sigmoid(-logits[tok_count:])[:, None] * slopes_real * score_vector
        + back_grad * score_vector * curves[tok_count:]
    ).astype(jnp.bfloat16)
    left_rows = jnp.concatenate([fake_rows, real_rows, r1_cot], 0)
    right_rows = jnp.concatenate([fake_cot, real_cot, lifted], 0)
    grad_term = lax.dot_general(
        left_rows, right_rows, (((0,), (0,)), ((), ())), preferred_element_type=jnp.float32
    )
    grad_shard = lax.psum_scatter(grad_term, "seq", scatter_dimension=0, tiled=True)
    return lax.psum(grad_shard, "grp")


def encode(v):
    head = v.astype(jnp.bfloat16)
    wide = head.astype(jnp.float32)
    scale = pl.reciprocal(jnp.maximum(jnp.abs(wide), 1e-30), approx=True) * STEPS
    q = jnp.clip(jnp.round((v - wide) * scale), -(LEVELS // 2), LEVELS // 2)
    n = v.shape[1] // 2
    return jnp.concatenate([head, (q[:, :n] * LEVELS + q[:, n:]).astype(jnp.bfloat16)], 1)


def decode(e):
    n = e.shape[1] // 3
    wide = e[:, : 2 * n].astype(jnp.float32)
    word = e[:, 2 * n :].astype(jnp.float32)
    first = jnp.round(word * (1.0 / LEVELS))
    q = jnp.concatenate([first, word - LEVELS * first], 1)
    return wide + jnp.abs(wide) * (q * (1.0 / STEPS))


def kernel(
    n_z, loss_scale,
    fake_ref, real_ref, w_ref, score_ref, out_ref,
    W, joined, tokT, tokP, igT, liftT, r1, r1T, r1P, R, RP, pre_s, slope_s, curve_s, gate_s,
    G, ex1, ey1, ex2, ey2, rx1, ry1, rx2, ry2, S, rz, ez, zf, A,
    w_s, w_r, wp_s, wp_r, tok_s, tok_r, r1_s, r1_r, R_s, R_r, g_s, g_r, z_s, z_r, zf_s, zf_r, a_s, a_r,
):
    f32 = jnp.float32
    bf16 = jnp.bfloat16
    rows, hid = w_ref.shape
    toks = fake_ref.shape[0]
    n_tiles = hid // TILE
    sub = TILE // 4
    hr = rows // 2
    zrow = zf.shape[2]
    xr = hr - zrow // 2
    g = lax.axis_index("grp")
    s = lax.axis_index("seq")
    y, x = g // 2, g % 2
    z, c = s // 2, s % 2
    gx, gy, gd = 2 * y + 1 - x, 2 * (1 - y) + x, 3 - g
    to_x = {"grp": gx, "seq": s}
    to_y = {"grp": gy, "seq": s}
    partner = {"grp": g, "seq": 2 * z + 1 - c}

    def to_z(zt):
        return {"grp": g, "seq": 2 * zt + c}

    barrier = pltpu.get_barrier_semaphore()
    greet = [to_x, to_y, partner] + [to_z((z + d) % n_z) for d in range(1, n_z)]
    for dev in greet:
        pl.semaphore_signal(barrier, inc=1, device_id=dev, device_id_type=MESH)
    pl.semaphore_wait(barrier, len(greet))

    pending = []

    def send(src, dst, ssem, rsem, dev):
        cp = pltpu.make_async_remote_copy(
            src_ref=src, dst_ref=dst, send_sem=ssem, recv_sem=rsem, device_id=dev, device_id_type=MESH
        )
        cp.start()
        pending.append(cp)

    def arrived(ref, rsem):
        pltpu.make_async_remote_copy(
            src_ref=ref, dst_ref=ref, send_sem=rsem, recv_sem=rsem, device_id=partner, device_id_type=MESH
        ).wait_recv()

    def rblk(seq):
        return pl.ds(pl.multiple_of(rows * seq, 16), rows)

    def rhalf(seq, h):
        return pl.ds(pl.multiple_of(rows * seq + hr * h, 16), hr)

    def quarter(j):
        return pl.ds(pl.multiple_of(j * TILE, TILE), TILE)

    def subq(t, j):
        return pl.ds(pl.multiple_of(t * TILE + j * sub, sub), sub)

    def tile(t):
        return pl.ds(t * TILE, TILE)

    order = [0, 2, 1] if n_z == 4 else list(range(n_z - 1))
    for t in range(n_tiles):
        for i in order:
            cols = subq(t, g)
            send(
                w_ref.at[:, cols], W.at[rblk(s), cols], w_s.at[t, i, 0], w_r.at[t, i, 0],
                to_z((z + 1 + i) % n_z),
            )
        send(w_ref.at[:, tile(t)], W.at[rblk(s), tile(t)], wp_s.at[t, n_z - 1], wp_r.at[t, n_z - 1], partner)
    W[rblk(s), :] = w_ref[...]
    joined[0:toks, :] = fake_ref[...]
    joined[toks : 2 * toks, :] = real_ref[...]
    igT[...] = jnp.zeros_like(igT)
    gate_s[...] = jnp.zeros_like(gate_s)

    @pl.loop(0, joined.shape[1] // TILE)
    def _(t):
        cols = pl.ds(pl.multiple_of(t * TILE, TILE), TILE)
        tokT[cols, :] = joined[:, cols].T

    def zseq(i, parity):
        return 2 * ((z + n_z - 1 - i) % n_z) + parity

    def stage_a(t):
        for i in order:
            mine = W.at[rblk(zseq(i, c)), subq(t, g)]
            arrived(mine, w_r.at[t, i, 0])
            send(mine, mine, w_s.at[t, i, 1], w_r.at[t, i, 1], to_x)
            send(mine, mine, w_s.at[t, i, 2], w_r.at[t, i, 2], to_y)

    def stage_b(t):
        for i in order:
            sq = zseq(i, c)
            ref = W.at[rblk(sq), subq(t, gx)]
            arrived(ref, w_r.at[t, i, 1])
            h = W.at[rhalf(sq, 0), subq(t, gx)]
            send(h, h, w_s.at[t, i, 3], w_r.at[t, i, 3], to_y)
            ref = W.at[rblk(sq), subq(t, gy)]
            arrived(ref, w_r.at[t, i, 2])
            h = W.at[rhalf(sq, 1), subq(t, gy)]
            send(h, h, w_s.at[t, i, 4], w_r.at[t, i, 4], to_x)

    def stage_c(t):
        for i in order:
            sq = zseq(i, c)
            arrived(W.at[rhalf(sq, 0), subq(t, gd)], w_r.at[t, i, 3])
            arrived(W.at[rhalf(sq, 1), subq(t, gd)], w_r.at[t, i, 4])
            ref = W.at[rblk(sq), tile(t)]
            send(ref, ref, wp_s.at[t, i], wp_r.at[t, i], partner)

    def stage_d(t):
        arrived(W.at[rblk(2 * z + 1 - c), tile(t)], wp_r.at[t, n_z - 1])
        for i in order:
            arrived(W.at[rblk(zseq(i, 1 - c)), tile(t)], wp_r.at[t, i])

    def lanes(v):
        out = v[:, 0:128]
        for q in range(1, TILE // 128):
            out = out + v[:, 128 * q : 128 * q + 128]
        return out

    def forward(t):
        cols = tile(t)
        pre_s[...] = jnp.dot(joined[...], W[:, cols], preferred_element_type=f32)

        def common(ch):
            sv = score_ref[:, cols]
            pre = pre_s[ch, :]
            sig = 1.0 / (1.0 + jnp.exp(-pre))
            gate_s[ch, :] += lanes(pre * sig * sv)
            sl = sig * (1.0 + pre * (1.0 - sig)) * sv
            slope_s[ch, cols] = sl
            return sv, pre, sig, sl

        @pl.loop(0, toks // CHUNK)
        def _(u):
            common(pl.ds(pl.multiple_of(u * CHUNK, CHUNK), CHUNK))

        @pl.loop(0, toks // CHUNK)
        def _(u):
            ch = pl.ds(pl.multiple_of(u * CHUNK, CHUNK), CHUNK)
            sv, pre, sig, sl = common(pl.ds(pl.multiple_of(toks + u * CHUNK, CHUNK), CHUNK))
            R[2, ch, cols] = sl.astype(bf16)
            curve_s[ch, cols] = sig * (1.0 - sig) * (2.0 + pre * (1.0 - 2.0 * sig)) * sv

        send(R.at[2, :, cols], RP.at[2, :, cols], R_s.at[2, t], R_r.at[2, t], partner)
        liftT[...] = R[2, :, cols].T

        @pl.loop(0, W.shape[0] // TILE)
        def _(u):
            ch = pl.ds(pl.multiple_of(u * TILE, TILE), TILE)
            igT[ch, :] += jnp.dot(W[ch, cols], liftT[...], preferred_element_type=f32)

    stage_a(0)
    for b in range(n_z):
        send(tokT.at[rblk(2 * b + 1 - c), :], tokP.at[b], tok_s.at[b], tok_r.at[b], partner)
    stage_b(0)
    for t in range(n_tiles):
        if t + 1 < n_tiles:
            stage_a(t + 1)
        stage_c(t)
        stage_d(t)
        forward(t)
        if t + 1 < n_tiles:
            stage_b(t + 1)

    @pl.loop(0, W.shape[0] // TILE)
    def _(t):
        cols = pl.ds(pl.multiple_of(t * TILE, TILE), TILE)
        r = (loss_scale * R1_WEIGHT * igT[cols, :]).astype(bf16)
        r1T[cols, :] = r
        r1[:, cols] = r.T

    for b in range(n_z):
        send(r1T.at[rblk(2 * b + 1 - c), :], r1P.at[b], r1_s.at[b], r1_r.at[b], partner)

    gate = jnp.sum(gate_s[...], axis=1, keepdims=True)
    gate_s[0:toks, :] = jnp.broadcast_to(loss_scale / (1.0 + jnp.exp(-gate[:toks])), (toks, 128))
    gate_s[toks : 2 * toks, :] = jnp.broadcast_to(-loss_scale / (1.0 + jnp.exp(gate[toks:])), (toks, 128))

    def gated(ch, cols):
        return jnp.concatenate([gate_s[ch, :]] * (TILE // 128), 1) * slope_s[ch, cols]

    for t in range(n_tiles):
        cols = tile(t)
        pre_s[0:toks, :] = jnp.dot(r1[...], W[:, cols], preferred_element_type=f32)

        @pl.loop(0, toks // CHUNK)
        def _(u):
            ch = pl.ds(pl.multiple_of(u * CHUNK, CHUNK), CHUNK)
            R[0, ch, cols] = gated(ch, cols).astype(bf16)
            low = pl.ds(pl.multiple_of(toks + u * CHUNK, CHUNK), CHUNK)
            R[1, ch, cols] = (gated(low, cols) + pre_s[ch, :] * curve_s[ch, cols]).astype(bf16)

        send(R.at[0:2, :, cols], RP.at[0:2, :, cols], R_s.at[0, t], R_r.at[0, t], partner)

    for b in range(n_z):
        arrived(tokP.at[b], tok_r.at[b])
        arrived(r1P.at[b], r1_r.at[b])
    for t in range(n_tiles):
        arrived(RP.at[2, :, tile(t)], R_r.at[2, t])
        arrived(RP.at[0:2, :, tile(t)], R_r.at[0, t])

    last = n_z - 1
    hops = [2, 1, 3, 0] if n_z == 4 else [(1 + k) % n_z for k in range(n_z)]

    def block(k):
        zb = (z + hops[k]) % n_z
        mine = rblk(2 * zb + c)

        @pl.loop(0, n_tiles)
        def _(t):
            cols = pl.ds(pl.multiple_of(t * TILE, TILE), TILE)
            acc = jnp.dot(tokT[mine, :], R[0:2, :, cols].reshape(2 * toks, TILE), preferred_element_type=f32)
            acc += jnp.dot(r1T[mine, :], R[2, :, cols], preferred_element_type=f32)
            acc += jnp.dot(tokP[zb], RP[0:2, :, cols].reshape(2 * toks, TILE), preferred_element_type=f32)
            acc += jnp.dot(r1P[zb], RP[2, :, cols], preferred_element_type=f32)
            G[k, :, cols] = acc

        if k < last:
            for t in range(n_tiles):
                for u in range(0, zrow, CHUNK):
                    ez[k, t, u : u + CHUNK, :] = encode(G[k, xr + u : xr + u + CHUNK, tile(t)])
            send(ez.at[k], zf.at[k], zf_s.at[k], zf_r.at[k], to_z(zb))

    def over(m, body):
        @pl.loop(0, m // CHUNK)
        def _(u):
            body(pl.multiple_of(u * CHUNK, CHUNK))

    def at(start):
        return pl.ds(pl.multiple_of(start, CHUNK), CHUNK)

    def spans(k):
        if k < last:
            return 0, xr + zrow, xr
        return 0, hr, hr

    def step1(k):
        bx, by, m = spans(k)
        if k == last:
            for i in range(last):
                arrived(zf.at[i], zf_r.at[i])
            for t in range(n_tiles):
                for u in range(0, zrow, CHUNK):
                    mid = G[k, xr + u : xr + u + CHUNK, tile(t)]
                    for i in range(last):
                        mid = mid + decode(zf[i, t, u : u + CHUNK, :])
                    G[k, xr + u : xr + u + CHUNK, tile(t)] = mid
        for j in range(2):
            def put_x(r):
                ex1[k, j, at(r), :] = encode(G[k, at(bx + r), quarter(2 * j + 1 - x)])

            over(m, put_x)
            part = pl.ds(0, m)
            send(ex1.at[k, j, part], rx1.at[k, j, part], g_s.at[k, j], g_r.at[k, j], to_x)

            def put_y(r):
                ey1[k, j, at(r), :] = encode(G[k, at(by + r), quarter(2 * (1 - y) + j)])

            over(m, put_y)
            send(ey1.at[k, j, part], ry1.at[k, j, part], g_s.at[k, 2 + j], g_r.at[k, 2 + j], to_y)

    def step2(k):
        bx, by, m = spans(k)
        part = pl.ds(0, m)
        for j in range(2):
            arrived(rx1.at[k, j, part], g_r.at[k, j])
            arrived(ry1.at[k, j, part], g_r.at[k, 2 + j])

        def put_x(r):
            ex2[k, at(r), :] = encode(G[k, at(bx + r), quarter(gy)] + decode(rx1[k, 1 - y, at(r), :]))

        over(m, put_x)
        send(ex2.at[k, part], rx2.at[k, part], g_s.at[k, 4], g_r.at[k, 4], to_y)

        def put_y(r):
            ey2[k, at(r), :] = encode(G[k, at(by + r), quarter(gx)] + decode(ry1[k, 1 - x, at(r), :]))

        over(m, put_y)
        send(ey2.at[k, part], ry2.at[k, part], g_s.at[k, 5], g_r.at[k, 5], to_x)

    def step3(k):
        bx, by, m = spans(k)
        arrived(rx2.at[k, pl.ds(0, m)], g_r.at[k, 4])
        arrived(ry2.at[k, pl.ds(0, m)], g_r.at[k, 5])

        def sum_x(r):
            return G[k, at(bx + r), quarter(g)] + decode(rx1[k, y, at(r), :]) + decode(rx2[k, at(r), :])

        def sum_y(r):
            return G[k, at(by + r), quarter(g)] + decode(ry1[k, x, at(r), :]) + decode(ry2[k, at(r), :])

        if k < last:
            def put(r):
                S[k, at(r), :] = encode(sum_x(r))
                S[k, at(xr + r), :] = encode(sum_y(r))

            over(m, put)
            send(S.at[k], rz.at[k], z_s.at[k], z_r.at[k], to_z((z + hops[k]) % n_z))
        else:
            def far(r):
                out = decode(rz[0, at(r), :])
                for i in range(1, last):
                    out = out + decode(rz[i, at(r), :])
                return out

            def both(r):
                A[g, at(r), :] = encode(sum_x(r) + far(r))
                A[g, at(xr + zrow + r), :] = encode(sum_y(xr + zrow - hr + r) + far(xr + r))

            def only(r):
                A[g, at(xr + r), :] = encode(sum_x(xr + r))
                A[g, at(hr + r), :] = encode(sum_y(r))

            over(xr, both)
            over(zrow // 2, only)

    def unpack(j):
        def put(r):
            out_ref[at(r), quarter(j)] = decode(A[j, at(r), :])

        over(rows, put)

    for k in range(n_z):
        block(k)
        if k < last:
            step1(k)
        if k >= 2:
            step2(k - 2)
    step1(last)
    step3(0)
    step2(last - 1)
    for k in range(1, last):
        step3(k)
    step2(last)
    for k in range(last):
        arrived(rz.at[k], z_r.at[k])
    step3(last)
    send(A.at[g], A.at[g], a_s.at[0], a_r.at[0], to_x)
    send(A.at[g], A.at[g], a_s.at[1], a_r.at[1], to_y)
    unpack(g)
    lo, hi = pl.ds(0, hr), pl.ds(hr, hr)
    arrived(A.at[gx], a_r.at[0])
    send(A.at[gx, lo], A.at[gx, lo], a_s.at[2], a_r.at[2], to_y)
    arrived(A.at[gy], a_r.at[1])
    send(A.at[gy, hi], A.at[gy, hi], a_s.at[3], a_r.at[3], to_x)
    unpack(gx)
    unpack(gy)
    arrived(A.at[gd, lo], a_r.at[2])
    arrived(A.at[gd, hi], a_r.at[3])
    unpack(gd)
    for cp in pending:
        cp.wait_send()


def fused(n_z, loss_scale, fake_tokens, real_tokens, proj_weight, score_vector):
    toks, d_in = fake_tokens.shape[1:]
    rows, hid = proj_weight.shape
    f32, bf16 = jnp.float32, jnp.bfloat16
    vm, dma = pltpu.VMEM, pltpu.SemaphoreType.DMA
    tiles = hid // TILE
    hr = rows // 2
    zrow = rows // 6
    xr = hr - zrow // 2
    scratch = [
        vm((d_in, hid), bf16),
        vm((2 * toks, d_in), bf16),
        vm((d_in, 2 * toks), bf16),
        vm((n_z, rows, 2 * toks), bf16),
        vm((d_in, toks), f32),
        vm((TILE, toks), bf16),
        vm((toks, d_in), bf16),
        vm((d_in, toks), bf16),
        vm((n_z, rows, toks), bf16),
        vm((3, toks, hid), bf16),
        vm((3, toks, hid), bf16),
        vm((2 * toks, TILE), f32),
        vm((2 * toks, hid), f32),
        vm((toks, hid), f32),
        vm((2 * toks, 128), f32),
        vm((n_z, rows, hid), f32),
        vm((n_z, 2, hr, CODED), bf16),
        vm((n_z, 2, hr, CODED), bf16),
        vm((n_z, hr, CODED), bf16),
        vm((n_z, hr, CODED), bf16),
        vm((n_z, 2, hr, CODED), bf16),
        vm((n_z, 2, hr, CODED), bf16),
        vm((n_z, hr, CODED), bf16),
        vm((n_z, hr, CODED), bf16),
        vm((n_z - 1, 2 * xr, CODED), bf16),
        vm((n_z - 1, 2 * xr, CODED), bf16),
        vm((n_z - 1, tiles, zrow, CODED), bf16),
        vm((n_z - 1, tiles, zrow, CODED), bf16),
        vm((4, rows, CODED), bf16),
        dma((tiles, n_z - 1, 5)), dma((tiles, n_z - 1, 5)),
        dma((tiles, n_z)), dma((tiles, n_z)),
        dma((n_z,)), dma((n_z,)),
        dma((n_z,)), dma((n_z,)),
        dma((3, tiles)), dma((3, tiles)),
        dma((n_z, 6)), dma((n_z, 6)),
        dma((n_z - 1,)), dma((n_z - 1,)),
        dma((n_z - 1,)), dma((n_z - 1,)),
        dma((4,)), dma((4,)),
    ]
    return pl.pallas_call(
        functools.partial(kernel, n_z, loss_scale),
        out_shape=jax.ShapeDtypeStruct((rows, hid), f32),
        in_specs=[pl.BlockSpec(memory_space=pltpu.VMEM)] * 4,
        out_specs=pl.BlockSpec(memory_space=pltpu.VMEM),
        scratch_shapes=scratch,
        compiler_params=pltpu.CompilerParams(
            collective_id=0, has_side_effects=True, vmem_limit_bytes=58 * 1024 * 1024
        ),
    )(fake_tokens[0], real_tokens[0], proj_weight, score_vector[None, :])


def solution(mesh):
    in_specs = (P("grp", "seq", None), P("grp", "seq", None), P("seq", None), P())
    out_specs = P("seq", None)
    n_grp, n_seq = mesh.shape["grp"], mesh.shape["seq"]

    def body(fake_tokens, real_tokens, proj_weight, score_vector):
        toks = fake_tokens.shape[1]
        rows, hid = proj_weight.shape
        fits = n_grp == 4 and n_seq == 8 and hid == 4 * TILE and rows % 192 == 0 and toks % 64 == 0
        if not fits:
            return per_device(fake_tokens, real_tokens, proj_weight, score_vector)
        loss_scale = math.sqrt(hid / (n_grp * n_seq * toks))
        return fused(n_seq // 2, loss_scale, fake_tokens, real_tokens, proj_weight, score_vector)

    return jax.shard_map(body, mesh=mesh, in_specs=in_specs, out_specs=out_specs, check_vma=False)
```

```python
import functools
import math

import jax
import jax.numpy as jnp
from jax import lax
from jax.experimental import pallas as pl
from jax.experimental.pallas import tpu as pltpu
from jax.sharding import PartitionSpec as P

R1_WEIGHT = 40.0
MESH = pl.DeviceIdType.MESH
TILE = 512
CHUNK = 16
CODED = TILE + TILE // 2
LEVELS = 21
STEPS = 2560.0


def per_device(fake_tokens, real_tokens, proj_weight, score_vector):
    fake_rows = fake_tokens[0]
    real_rows = real_tokens[0]
    tok_count = fake_rows.shape[0]
    hid_width = proj_weight.shape[1]
    loss_scale = math.sqrt(hid_width / (lax.axis_size("grp") * lax.axis_size("seq") * tok_count))
    joined = jnp.concatenate([fake_rows, real_rows], 0)
    full_weight = lax.all_gather(proj_weight, "seq", axis=0, tiled=True)
    preact = jnp.dot(joined, full_weight, preferred_element_type=jnp.float32)
    squash = jax.nn.sigmoid(preact)
    slopes = squash * (1.0 + preact * (1.0 - squash))
    curves = squash * (1.0 - squash) * (2.0 + preact * (1.0 - 2.0 * squash))
    logits = jnp.dot(preact * squash, score_vector, precision=lax.Precision.HIGHEST)
    slopes_real = slopes[tok_count:]
    lifted = (slopes_real * score_vector).astype(jnp.bfloat16)
    input_grad = lax.dot_general(
        lifted, full_weight, (((1,), (1,)), ((), ())), preferred_element_type=jnp.float32
    )
    r1_cot = (loss_scale * R1_WEIGHT * input_grad).astype(jnp.bfloat16)
    back_grad = jnp.dot(r1_cot, full_weight, preferred_element_type=jnp.float32)
    fake_cot = (
        loss_scale * jax.nn.sigmoid(logits[:tok_count])[:, None] * slopes[:tok_count] * score_vector
    ).astype(jnp.bfloat16)
    real_cot = (
        -loss_scale * jax.nn.sigmoid(-logits[tok_count:])[:, None] * slopes_real * score_vector
        + back_grad * score_vector * curves[tok_count:]
    ).astype(jnp.bfloat16)
    left_rows = jnp.concatenate([fake_rows, real_rows, r1_cot], 0)
    right_rows = jnp.concatenate([fake_cot, real_cot, lifted], 0)
    grad_term = lax.dot_general(
        left_rows, right_rows, (((0,), (0,)), ((), ())), preferred_element_type=jnp.float32
    )
    grad_shard = lax.psum_scatter(grad_term, "seq", scatter_dimension=0, tiled=True)
    return lax.psum(grad_shard, "grp")


def encode(v):
    head = v.astype(jnp.bfloat16)
    wide = head.astype(jnp.float32)
    scale = pl.reciprocal(jnp.maximum(jnp.abs(wide), 1e-30), approx=True) * STEPS
    q = jnp.round((v - wide) * scale)
    n = v.shape[1] // 2
    return jnp.concatenate([head, (q[:, :n] * LEVELS + q[:, n:]).astype(jnp.bfloat16)], 1)


def decode(e):
    n = e.shape[1] // 3
    wide = e[:, : 2 * n].astype(jnp.float32)
    word = e[:, 2 * n :].astype(jnp.float32)
    first = jnp.round(word * (1.0 / LEVELS))
    q = jnp.concatenate([first, word - LEVELS * first], 1)
    return wide + jnp.abs(wide) * (q * (1.0 / STEPS))


def kernel(
    n_z, loss_scale,
    fake_ref, real_ref, w_ref, score_ref, out_ref,
    W, joined, tokT, tokP, igT, liftT, r1, r1T, r1P, R, RP, pre_s, slope_s, curve_s, gate_s,
    G, ex1, ey1, ex2, ey2, rx1, ry1, rx2, ry2, S, rz, ez, zf, A,
    w_s, w_r, wp_s, wp_r, tok_s, tok_r, r1_s, r1_r, R_s, R_r, g_s, g_r, z_s, z_r, zf_s, zf_r, a_s, a_r,
):
    f32 = jnp.float32
    bf16 = jnp.bfloat16
    rows, hid = w_ref.shape
    toks = fake_ref.shape[0]
    n_tiles = hid // TILE
    sub = TILE // 4
    hr = rows // 2
    zrow = zf.shape[2]
    xr = hr - zrow // 2
    g = lax.axis_index("grp")
    s = lax.axis_index("seq")
    y, x = g // 2, g % 2
    z, c = s // 2, s % 2
    gx, gy, gd = 2 * y + 1 - x, 2 * (1 - y) + x, 3 - g
    to_x = {"grp": gx, "seq": s}
    to_y = {"grp": gy, "seq": s}
    partner = {"grp": g, "seq": 2 * z + 1 - c}

    def to_z(zt):
        return {"grp": g, "seq": 2 * zt + c}

    barrier = pltpu.get_barrier_semaphore()
    greet = [to_x, to_y, partner] + [to_z((z + d) % n_z) for d in range(1, n_z)]
    for dev in greet:
        pl.semaphore_signal(barrier, inc=1, device_id=dev, device_id_type=MESH)
    pl.semaphore_wait(barrier, len(greet))

    pending = []

    def send(src, dst, ssem, rsem, dev, keep=False):
        cp = pltpu.make_async_remote_copy(
            src_ref=src, dst_ref=dst, send_sem=ssem, recv_sem=rsem, device_id=dev, device_id_type=MESH
        )
        cp.start()
        if keep:
            pending.append(cp)

    def arrived(ref, rsem):
        pltpu.make_async_remote_copy(
            src_ref=ref, dst_ref=ref, send_sem=rsem, recv_sem=rsem, device_id=partner, device_id_type=MESH
        ).wait_recv()

    def sent(ref, ssem):
        pltpu.make_async_remote_copy(
            src_ref=ref, dst_ref=ref, send_sem=ssem, recv_sem=ssem, device_id=partner, device_id_type=MESH
        ).wait_send()

    def rblk(seq):
        return pl.ds(pl.multiple_of(rows * seq, 16), rows)

    def rhalf(seq, h):
        return pl.ds(pl.multiple_of(rows * seq + hr * h, 16), hr)

    def quarter(j):
        return pl.ds(pl.multiple_of(j * TILE, TILE), TILE)

    def subq(t, j):
        return pl.ds(pl.multiple_of(t * TILE + j * sub, sub), sub)

    def tile(t):
        return pl.ds(pl.multiple_of(t * TILE, TILE), TILE)

    order = [0, 2, 1] if n_z == 4 else list(range(n_z - 1))
    @pl.loop(0, n_tiles)
    def _(t):
        for i in order:
            cols = subq(t, g)
            send(
                w_ref.at[:, cols], W.at[rblk(s), cols], w_s.at[t, i, 0], w_r.at[t, i, 0],
                to_z((z + 1 + i) % n_z),
            )
        send(w_ref.at[:, tile(t)], W.at[rblk(s), tile(t)], wp_s.at[t, n_z - 1], wp_r.at[t, n_z - 1], partner)
    W[rblk(s), :] = w_ref[...]
    joined[0:toks, :] = fake_ref[...]
    joined[toks : 2 * toks, :] = real_ref[...]
    igT[...] = jnp.zeros_like(igT)
    gate_s[...] = jnp.zeros_like(gate_s)

    @pl.loop(0, joined.shape[1] // TILE)
    def _(t):
        cols = pl.ds(pl.multiple_of(t * TILE, TILE), TILE)
        tokT[cols, :] = joined[:, cols].T

    def zseq(i, parity):
        return 2 * ((z + n_z - 1 - i) % n_z) + parity

    def stage_a(t):
        for i in order:
            mine = W.at[rblk(zseq(i, c)), subq(t, g)]
            arrived(mine, w_r.at[t, i, 0])
            send(mine, mine, w_s.at[t, i, 1], w_r.at[t, i, 1], to_x)
            send(mine, mine, w_s.at[t, i, 2], w_r.at[t, i, 2], to_y)

    def stage_b(t):
        for i in order:
            sq = zseq(i, c)
            ref = W.at[rblk(sq), subq(t, gx)]
            arrived(ref, w_r.at[t, i, 1])
            h = W.at[rhalf(sq, 0), subq(t, gx)]
            send(h, h, w_s.at[t, i, 3], w_r.at[t, i, 3], to_y)
            ref = W.at[rblk(sq), subq(t, gy)]
            arrived(ref, w_r.at[t, i, 2])
            h = W.at[rhalf(sq, 1), subq(t, gy)]
            send(h, h, w_s.at[t, i, 4], w_r.at[t, i, 4], to_x)

    def stage_c(t):
        for i in order:
            sq = zseq(i, c)
            arrived(W.at[rhalf(sq, 0), subq(t, gd)], w_r.at[t, i, 3])
            arrived(W.at[rhalf(sq, 1), subq(t, gd)], w_r.at[t, i, 4])
            ref = W.at[rblk(sq), tile(t)]
            send(ref, ref, wp_s.at[t, i], wp_r.at[t, i], partner)

    def stage_d(t):
        arrived(W.at[rblk(2 * z + 1 - c), tile(t)], wp_r.at[t, n_z - 1])
        for i in order:
            arrived(W.at[rblk(zseq(i, 1 - c)), tile(t)], wp_r.at[t, i])

    def lanes(v):
        out = v[:, 0:128]
        for q in range(1, TILE // 128):
            out = out + v[:, 128 * q : 128 * q + 128]
        return out

    def forward(t):
        cols = tile(t)
        pre_s[...] = jnp.dot(joined[...], W[:, cols], preferred_element_type=f32)

        def common(ch):
            sv = score_ref[:, cols]
            pre = pre_s[ch, :]
            sig = 1.0 / (1.0 + jnp.exp(-pre))
            gate_s[ch, :] += lanes(pre * sig * sv)
            sl = sig * (1.0 + pre * (1.0 - sig)) * sv
            slope_s[ch, cols] = sl
            return sv, pre, sig, sl

        @pl.loop(0, toks // CHUNK)
        def _(u):
            common(pl.ds(pl.multiple_of(u * CHUNK, CHUNK), CHUNK))

        @pl.loop(0, toks // CHUNK)
        def _(u):
            ch = pl.ds(pl.multiple_of(u * CHUNK, CHUNK), CHUNK)
            sv, pre, sig, sl = common(pl.ds(pl.multiple_of(toks + u * CHUNK, CHUNK), CHUNK))
            R[2, ch, cols] = sl.astype(bf16)
            curve_s[ch, cols] = sig * (1.0 - sig) * (2.0 + pre * (1.0 - 2.0 * sig)) * sv

        send(R.at[2, :, cols], RP.at[2, :, cols], R_s.at[2, t], R_r.at[2, t], partner)
        liftT[...] = R[2, :, cols].T

        @pl.loop(0, W.shape[0] // TILE)
        def _(u):
            ch = pl.ds(pl.multiple_of(u * TILE, TILE), TILE)
            igT[ch, :] += jnp.dot(W[ch, cols], liftT[...], preferred_element_type=f32)

    stage_a(0)
    for b in range(n_z):
        send(tokT.at[rblk(2 * b + 1 - c), :], tokP.at[b], tok_s.at[b], tok_r.at[b], partner, True)
    stage_b(0)

    @pl.loop(0, n_tiles)
    def _(t):
        @pl.when(t + 1 < n_tiles)
        def _():
            stage_a(t + 1)

        stage_c(t)
        stage_d(t)
        forward(t)

        @pl.when(t + 1 < n_tiles)
        def _():
            stage_b(t + 1)

    @pl.loop(0, W.shape[0] // TILE)
    def _(t):
        cols = pl.ds(pl.multiple_of(t * TILE, TILE), TILE)
        r = (loss_scale * R1_WEIGHT * igT[cols, :]).astype(bf16)
        r1T[cols, :] = r
        r1[:, cols] = r.T

    for b in range(n_z):
        send(r1T.at[rblk(2 * b + 1 - c), :], r1P.at[b], r1_s.at[b], r1_r.at[b], partner, True)

    gate = jnp.sum(gate_s[...], axis=1, keepdims=True)
    gate_s[0:toks, :] = jnp.broadcast_to(loss_scale / (1.0 + jnp.exp(-gate[:toks])), (toks, 128))
    gate_s[toks : 2 * toks, :] = jnp.broadcast_to(-loss_scale / (1.0 + jnp.exp(gate[toks:])), (toks, 128))

    def gated(ch, cols):
        return jnp.concatenate([gate_s[ch, :]] * (TILE // 128), 1) * slope_s[ch, cols]

    @pl.loop(0, n_tiles)
    def _(t):
        cols = tile(t)
        pre_s[0:toks, :] = jnp.dot(r1[...], W[:, cols], preferred_element_type=f32)

        @pl.loop(0, toks // CHUNK)
        def _(u):
            ch = pl.ds(pl.multiple_of(u * CHUNK, CHUNK), CHUNK)
            R[0, ch, cols] = gated(ch, cols).astype(bf16)
            low = pl.ds(pl.multiple_of(toks + u * CHUNK, CHUNK), CHUNK)
            R[1, ch, cols] = (gated(low, cols) + pre_s[ch, :] * curve_s[ch, cols]).astype(bf16)

        send(R.at[0:2, :, cols], RP.at[0:2, :, cols], R_s.at[0, t], R_r.at[0, t], partner)

    for b in range(n_z):
        arrived(tokP.at[b], tok_r.at[b])
        arrived(r1P.at[b], r1_r.at[b])
    @pl.loop(0, n_tiles)
    def _(t):
        arrived(RP.at[2, :, tile(t)], R_r.at[2, t])
        arrived(RP.at[0:2, :, tile(t)], R_r.at[0, t])

    last = n_z - 1

    def hop(k):
        return (z + 1 + k) % n_z

    def block(k, own=False):
        zb = hop(k)
        mine = rblk(2 * zb + c)

        @pl.loop(0, n_tiles)
        def _(t):
            cols = pl.ds(pl.multiple_of(t * TILE, TILE), TILE)
            acc = jnp.dot(tokT[mine, :], R[0:2, :, cols].reshape(2 * toks, TILE), preferred_element_type=f32)
            acc += jnp.dot(r1T[mine, :], R[2, :, cols], preferred_element_type=f32)
            acc += jnp.dot(tokP[zb], RP[0:2, :, cols].reshape(2 * toks, TILE), preferred_element_type=f32)
            acc += jnp.dot(r1P[zb], RP[2, :, cols], preferred_element_type=f32)
            G[k, :, cols] = acc

        if not own:
            @pl.loop(0, n_tiles)
            def _(t):
                for u in range(0, zrow, CHUNK):
                    ez[k, t, u : u + CHUNK, :] = encode(G[k, xr + u : xr + u + CHUNK, tile(t)])

            send(ez.at[k], zf.at[k], zf_s.at[k], zf_r.at[k], to_z(zb))

    def over(m, body):
        @pl.loop(0, m // CHUNK)
        def _(u):
            body(pl.multiple_of(u * CHUNK, CHUNK))

    def at(start):
        return pl.ds(pl.multiple_of(start, CHUNK), CHUNK)

    def spans(own):
        if not own:
            return 0, xr + zrow, xr
        return 0, hr, hr

    def step1(k, own=False):
        bx, by, m = spans(own)
        if own:
            for i in range(last):
                arrived(zf.at[i], zf_r.at[i])

            @pl.loop(0, n_tiles)
            def _(t):
                for u in range(0, zrow, CHUNK):
                    mid = G[k, xr + u : xr + u + CHUNK, tile(t)]
                    for i in range(last):
                        mid = mid + decode(zf[i, t, u : u + CHUNK, :])
                    G[k, xr + u : xr + u + CHUNK, tile(t)] = mid
        for j in range(2):
            def put_x(r):
                ex1[k, j, at(r), :] = encode(G[k, at(bx + r), quarter(2 * j + 1 - x)])

            over(m, put_x)
            part = pl.ds(0, m)
            send(ex1.at[k, j, part], rx1.at[k, j, part], g_s.at[k, j], g_r.at[k, j], to_x)

            def put_y(r):
                ey1[k, j, at(r), :] = encode(G[k, at(by + r), quarter(2 * (1 - y) + j)])

            over(m, put_y)
            send(ey1.at[k, j, part], ry1.at[k, j, part], g_s.at[k, 2 + j], g_r.at[k, 2 + j], to_y)

    def step2(k, own=False):
        bx, by, m = spans(own)
        part = pl.ds(0, m)
        for j in range(2):
            arrived(rx1.at[k, j, part], g_r.at[k, j])
            arrived(ry1.at[k, j, part], g_r.at[k, 2 + j])

        def put_x(r):
            ex2[k, at(r), :] = encode(G[k, at(bx + r), quarter(gy)] + decode(rx1[k, 1 - y, at(r), :]))

        over(m, put_x)
        send(ex2.at[k, part], rx2.at[k, part], g_s.at[k, 4], g_r.at[k, 4], to_y)

        def put_y(r):
            ey2[k, at(r), :] = encode(G[k, at(by + r), quarter(gx)] + decode(ry1[k, 1 - x, at(r), :]))

        over(m, put_y)
        send(ey2.at[k, part], ry2.at[k, part], g_s.at[k, 5], g_r.at[k, 5], to_x)

    def step3(k, own=False):
        bx, by, m = spans(own)
        arrived(rx2.at[k, pl.ds(0, m)], g_r.at[k, 4])
        arrived(ry2.at[k, pl.ds(0, m)], g_r.at[k, 5])

        def sum_x(r):
            return G[k, at(bx + r), quarter(g)] + decode(rx1[k, y, at(r), :]) + decode(rx2[k, at(r), :])

        def sum_y(r):
            return G[k, at(by + r), quarter(g)] + decode(ry1[k, x, at(r), :]) + decode(ry2[k, at(r), :])

        if not own:
            def put(r):
                S[k, at(r), :] = encode(sum_x(r))
                S[k, at(xr + r), :] = encode(sum_y(r))

            over(m, put)
            send(S.at[k], rz.at[k], z_s.at[k], z_r.at[k], to_z(hop(k)))
        else:
            def far(r):
                out = decode(rz[0, at(r), :])
                for i in range(1, last):
                    out = out + decode(rz[i, at(r), :])
                return out

            def both(r):
                A[g, at(r), :] = encode(sum_x(r) + far(r))
                A[g, at(xr + zrow + r), :] = encode(sum_y(xr + zrow - hr + r) + far(xr + r))

            def only(r):
                A[g, at(xr + r), :] = encode(sum_x(xr + r))
                A[g, at(hr + r), :] = encode(sum_y(r))

            over(xr, both)
            over(zrow // 2, only)

    def unpack(j):
        def put(r):
            out_ref[at(r), quarter(j)] = decode(A[j, at(r), :])

        over(rows, put)

    @pl.loop(0, last)
    def _(k):
        block(k)
        step1(k)

        @pl.when(k >= 1)
        def _():
            step2(k - 1)

    block(last, True)
    step1(last, True)

    @pl.loop(0, last)
    def _(k):
        @pl.when(k == 1)
        def _():
            step2(last - 1)

        step3(k)

    step2(last, True)
    for k in range(last):
        arrived(rz.at[k], z_r.at[k])
    step3(last, True)
    send(A.at[g], A.at[g], a_s.at[0], a_r.at[0], to_x, True)
    send(A.at[g], A.at[g], a_s.at[1], a_r.at[1], to_y, True)
    unpack(g)
    lo, hi = pl.ds(0, hr), pl.ds(hr, hr)
    arrived(A.at[gx], a_r.at[0])
    send(A.at[gx, lo], A.at[gx, lo], a_s.at[2], a_r.at[2], to_y, True)
    arrived(A.at[gy], a_r.at[1])
    send(A.at[gy, hi], A.at[gy, hi], a_s.at[3], a_r.at[3], to_x, True)
    unpack(gx)
    unpack(gy)
    arrived(A.at[gd, lo], a_r.at[2])
    arrived(A.at[gd, hi], a_r.at[3])
    unpack(gd)
    for cp in pending:
        cp.wait_send()

    @pl.loop(0, n_tiles)
    def _(t):
        for i in order:
            for m in range(3):
                sent(W.at[0:rows, 0:sub], w_s.at[t, i, m])
            for m in range(3, 5):
                sent(W.at[0:hr, 0:sub], w_s.at[t, i, m])
        for i in range(n_z):
            sent(W.at[0:rows, 0:TILE], wp_s.at[t, i])
        sent(R.at[2, :, tile(t)], R_s.at[2, t])
        sent(R.at[0:2, :, tile(t)], R_s.at[0, t])

    def drain(k, own=False):
        part = pl.ds(0, spans(own)[2])
        for j in range(2):
            sent(ex1.at[k, j, part], g_s.at[k, j])
            sent(ey1.at[k, j, part], g_s.at[k, 2 + j])
        sent(ex2.at[k, part], g_s.at[k, 4])
        sent(ey2.at[k, part], g_s.at[k, 5])
        if not own:
            sent(ez.at[k], zf_s.at[k])
            sent(S.at[k], z_s.at[k])

    @pl.loop(0, last)
    def _(k):
        drain(k)

    drain(last, True)


def fused(n_z, loss_scale, fake_tokens, real_tokens, proj_weight, score_vector):
    toks, d_in = fake_tokens.shape[1:]
    rows, hid = proj_weight.shape
    f32, bf16 = jnp.float32, jnp.bfloat16
    vm, dma = pltpu.VMEM, pltpu.SemaphoreType.DMA
    tiles = hid // TILE
    hr = rows // 2
    zrow = rows // 6
    xr = hr - zrow // 2
    scratch = [
        vm((d_in, hid), bf16),
        vm((2 * toks, d_in), bf16),
        vm((d_in, 2 * toks), bf16),
        vm((n_z, rows, 2 * toks), bf16),
        vm((d_in, toks), f32),
        vm((TILE, toks), bf16),
        vm((toks, d_in), bf16),
        vm((d_in, toks), bf16),
        vm((n_z, rows, toks), bf16),
        vm((3, toks, hid), bf16),
        vm((3, toks, hid), bf16),
        vm((2 * toks, TILE), f32),
        vm((2 * toks, hid), f32),
        vm((toks, hid), f32),
        vm((2 * toks, 128), f32),
        vm((n_z, rows, hid), f32),
        vm((n_z, 2, hr, CODED), bf16),
        vm((n_z, 2, hr, CODED), bf16),
        vm((n_z, hr, CODED), bf16),
        vm((n_z, hr, CODED), bf16),
        vm((n_z, 2, hr, CODED), bf16),
        vm((n_z, 2, hr, CODED), bf16),
        vm((n_z, hr, CODED), bf16),
        vm((n_z, hr, CODED), bf16),
        vm((n_z - 1, 2 * xr, CODED), bf16),
        vm((n_z - 1, 2 * xr, CODED), bf16),
        vm((n_z - 1, tiles, zrow, CODED), bf16),
        vm((n_z - 1, tiles, zrow, CODED), bf16),
        vm((4, rows, CODED), bf16),
        dma((tiles, n_z - 1, 5)), dma((tiles, n_z - 1, 5)),
        dma((tiles, n_z)), dma((tiles, n_z)),
        dma((n_z,)), dma((n_z,)),
        dma((n_z,)), dma((n_z,)),
        dma((3, tiles)), dma((3, tiles)),
        dma((n_z, 6)), dma((n_z, 6)),
        dma((n_z - 1,)), dma((n_z - 1,)),
        dma((n_z - 1,)), dma((n_z - 1,)),
        dma((4,)), dma((4,)),
    ]
    return pl.pallas_call(
        functools.partial(kernel, n_z, loss_scale),
        out_shape=jax.ShapeDtypeStruct((rows, hid), f32),
        in_specs=[pl.BlockSpec(memory_space=pltpu.VMEM)] * 4,
        out_specs=pl.BlockSpec(memory_space=pltpu.VMEM),
        scratch_shapes=scratch,
        compiler_params=pltpu.CompilerParams(
            collective_id=0, has_side_effects=True, vmem_limit_bytes=58 * 1024 * 1024
        ),
    )(fake_tokens[0], real_tokens[0], proj_weight, score_vector[None, :])


def solution(mesh):
    in_specs = (P("grp", "seq", None), P("grp", "seq", None), P("seq", None), P())
    out_specs = P("seq", None)
    n_grp, n_seq = mesh.shape["grp"], mesh.shape["seq"]

    def body(fake_tokens, real_tokens, proj_weight, score_vector):
        toks = fake_tokens.shape[1]
        rows, hid = proj_weight.shape
        fits = n_grp == 4 and n_seq == 8 and hid == 4 * TILE and rows % 192 == 0 and toks % 64 == 0
        if not fits:
            return per_device(fake_tokens, real_tokens, proj_weight, score_vector)
        loss_scale = math.sqrt(hid / (n_grp * n_seq * toks))
        return fused(n_seq // 2, loss_scale, fake_tokens, real_tokens, proj_weight, score_vector)

    return jax.shard_map(body, mesh=mesh, in_specs=in_specs, out_specs=out_specs, check_vma=False)
```

```python
import functools
import math

import jax
import jax.numpy as jnp
from jax import lax
from jax.experimental import pallas as pl
from jax.experimental.pallas import tpu as pltpu
from jax.sharding import PartitionSpec as P

R1_WEIGHT = 40.0
MESH = pl.DeviceIdType.MESH
TILE = 512
CHUNK = 16
CODED = TILE + TILE // 2
LEVELS = 21
STEPS = 2560.0


def per_device(fake_tokens, real_tokens, proj_weight, score_vector):
    fake_rows = fake_tokens[0]
    real_rows = real_tokens[0]
    tok_count = fake_rows.shape[0]
    hid_width = proj_weight.shape[1]
    loss_scale = math.sqrt(hid_width / (lax.axis_size("grp") * lax.axis_size("seq") * tok_count))
    joined = jnp.concatenate([fake_rows, real_rows], 0)
    full_weight = lax.all_gather(proj_weight, "seq", axis=0, tiled=True)
    preact = jnp.dot(joined, full_weight, preferred_element_type=jnp.float32)
    squash = jax.nn.sigmoid(preact)
    slopes = squash * (1.0 + preact * (1.0 - squash))
    curves = squash * (1.0 - squash) * (2.0 + preact * (1.0 - 2.0 * squash))
    logits = jnp.dot(preact * squash, score_vector, precision=lax.Precision.HIGHEST)
    slopes_real = slopes[tok_count:]
    lifted = (slopes_real * score_vector).astype(jnp.bfloat16)
    input_grad = lax.dot_general(
        lifted, full_weight, (((1,), (1,)), ((), ())), preferred_element_type=jnp.float32
    )
    r1_cot = (loss_scale * R1_WEIGHT * input_grad).astype(jnp.bfloat16)
    back_grad = jnp.dot(r1_cot, full_weight, preferred_element_type=jnp.float32)
    fake_cot = (
        loss_scale * jax.nn.sigmoid(logits[:tok_count])[:, None] * slopes[:tok_count] * score_vector
    ).astype(jnp.bfloat16)
    real_cot = (
        -loss_scale * jax.nn.sigmoid(-logits[tok_count:])[:, None] * slopes_real * score_vector
        + back_grad * score_vector * curves[tok_count:]
    ).astype(jnp.bfloat16)
    left_rows = jnp.concatenate([fake_rows, real_rows, r1_cot], 0)
    right_rows = jnp.concatenate([fake_cot, real_cot, lifted], 0)
    grad_term = lax.dot_general(
        left_rows, right_rows, (((0,), (0,)), ((), ())), preferred_element_type=jnp.float32
    )
    grad_shard = lax.psum_scatter(grad_term, "seq", scatter_dimension=0, tiled=True)
    return lax.psum(grad_shard, "grp")


def encode(v):
    head = v.astype(jnp.bfloat16)
    wide = head.astype(jnp.float32)
    scale = pl.reciprocal(jnp.maximum(jnp.abs(wide), 1e-30), approx=True) * STEPS
    q = jnp.round((v - wide) * scale)
    n = v.shape[1] // 2
    return jnp.concatenate([head, (q[:, :n] * LEVELS + q[:, n:]).astype(jnp.bfloat16)], 1)


def decode(e):
    n = e.shape[1] // 3
    wide = e[:, : 2 * n].astype(jnp.float32)
    word = e[:, 2 * n :].astype(jnp.float32)
    first = jnp.round(word * (1.0 / LEVELS))
    q = jnp.concatenate([first, word - LEVELS * first], 1)
    return wide + jnp.abs(wide) * (q * (1.0 / STEPS))


def kernel(
    n_z, loss_scale,
    fake_ref, real_ref, w_ref, score_ref, out_ref,
    W, joined, tokT, L, igT, liftT, r1, r1T, R, pre_s, slope_s, curve_s, gate_s,
    G, ex1, ey1, ex2, ey2, rx1, ry1, rx2, ry2, S, rz, ez, zf, A,
    w_s, w_r, wp_s, wp_r, tok_s, tok_r, r1_s, r1_r, R_s, R_r, g_s, g_r, z_s, z_r, zf_s, zf_r, a_s, a_r,
):
    f32 = jnp.float32
    bf16 = jnp.bfloat16
    rows, hid = w_ref.shape
    toks = fake_ref.shape[0]
    n_tiles = hid // TILE
    pad = r1T.shape[1]
    lift, lift_p = 4 * toks, 4 * toks + pad
    sub = TILE // 4
    hr = rows // 2
    zrow = zf.shape[2]
    xr = hr - zrow // 2
    g = lax.axis_index("grp")
    s = lax.axis_index("seq")
    y, x = g // 2, g % 2
    z, c = s // 2, s % 2
    gx, gy, gd = 2 * y + 1 - x, 2 * (1 - y) + x, 3 - g
    to_x = {"grp": gx, "seq": s}
    to_y = {"grp": gy, "seq": s}
    partner = {"grp": g, "seq": 2 * z + 1 - c}

    def to_z(zt):
        return {"grp": g, "seq": 2 * zt + c}

    barrier = pltpu.get_barrier_semaphore()
    greet = [to_x, to_y, partner] + [to_z((z + d) % n_z) for d in range(1, n_z)]
    for dev in greet:
        pl.semaphore_signal(barrier, inc=1, device_id=dev, device_id_type=MESH)
    pl.semaphore_wait(barrier, len(greet))

    pending = []

    def send(src, dst, ssem, rsem, dev, keep=False):
        cp = pltpu.make_async_remote_copy(
            src_ref=src, dst_ref=dst, send_sem=ssem, recv_sem=rsem, device_id=dev, device_id_type=MESH
        )
        cp.start()
        if keep:
            pending.append(cp)

    def arrived(ref, rsem):
        pltpu.make_async_remote_copy(
            src_ref=ref, dst_ref=ref, send_sem=rsem, recv_sem=rsem, device_id=partner, device_id_type=MESH
        ).wait_recv()

    def sent(ref, ssem):
        pltpu.make_async_remote_copy(
            src_ref=ref, dst_ref=ref, send_sem=ssem, recv_sem=ssem, device_id=partner, device_id_type=MESH
        ).wait_send()

    def hop(k):
        return (z + 1 + k) % n_z

    def rblk(seq):
        return pl.ds(pl.multiple_of(rows * seq, 16), rows)

    def rhalf(seq, h):
        return pl.ds(pl.multiple_of(rows * seq + hr * h, 16), hr)

    def quarter(j):
        return pl.ds(pl.multiple_of(j * TILE, TILE), TILE)

    def subq(t, j):
        return pl.ds(pl.multiple_of(t * TILE + j * sub, sub), sub)

    def tile(t):
        return pl.ds(pl.multiple_of(t * TILE, TILE), TILE)

    order = [0, 2, 1] if n_z == 4 else list(range(n_z - 1))
    @pl.loop(0, n_tiles)
    def _(t):
        for i in order:
            cols = subq(t, g)
            send(
                w_ref.at[:, cols], W.at[rblk(s), cols], w_s.at[t, i, 0], w_r.at[t, i, 0],
                to_z((z + 1 + i) % n_z),
            )
        send(w_ref.at[:, tile(t)], W.at[rblk(s), tile(t)], wp_s.at[t, n_z - 1], wp_r.at[t, n_z - 1], partner)
    W[rblk(s), :] = w_ref[...]
    joined[0:toks, :] = fake_ref[...]
    joined[toks : 2 * toks, :] = real_ref[...]
    igT[...] = jnp.zeros_like(igT)
    r1T[:, toks:pad] = jnp.zeros((r1T.shape[0], pad - toks), bf16)
    R[lift + toks : lift_p, :] = jnp.zeros((pad - toks, hid), bf16)
    R[lift_p + toks : lift_p + pad, :] = jnp.zeros((pad - toks, hid), bf16)
    gate_s[...] = jnp.zeros_like(gate_s)

    @pl.loop(0, joined.shape[1] // TILE)
    def _(t):
        cols = pl.ds(pl.multiple_of(t * TILE, TILE), TILE)
        tokT[cols, :] = joined[:, cols].T

    def zseq(i, parity):
        return 2 * ((z + n_z - 1 - i) % n_z) + parity

    def stage_a(t):
        for i in order:
            mine = W.at[rblk(zseq(i, c)), subq(t, g)]
            arrived(mine, w_r.at[t, i, 0])
            send(mine, mine, w_s.at[t, i, 1], w_r.at[t, i, 1], to_x)
            send(mine, mine, w_s.at[t, i, 2], w_r.at[t, i, 2], to_y)

    def stage_b(t):
        for i in order:
            sq = zseq(i, c)
            ref = W.at[rblk(sq), subq(t, gx)]
            arrived(ref, w_r.at[t, i, 1])
            h = W.at[rhalf(sq, 0), subq(t, gx)]
            send(h, h, w_s.at[t, i, 3], w_r.at[t, i, 3], to_y)
            ref = W.at[rblk(sq), subq(t, gy)]
            arrived(ref, w_r.at[t, i, 2])
            h = W.at[rhalf(sq, 1), subq(t, gy)]
            send(h, h, w_s.at[t, i, 4], w_r.at[t, i, 4], to_x)

    def stage_c(t):
        for i in order:
            sq = zseq(i, c)
            arrived(W.at[rhalf(sq, 0), subq(t, gd)], w_r.at[t, i, 3])
            arrived(W.at[rhalf(sq, 1), subq(t, gd)], w_r.at[t, i, 4])
            ref = W.at[rblk(sq), tile(t)]
            send(ref, ref, wp_s.at[t, i], wp_r.at[t, i], partner)

    def stage_d(t):
        arrived(W.at[rblk(2 * z + 1 - c), tile(t)], wp_r.at[t, n_z - 1])
        for i in order:
            arrived(W.at[rblk(zseq(i, 1 - c)), tile(t)], wp_r.at[t, i])

    def lanes(v):
        out = v[:, 0:128]
        for q in range(1, TILE // 128):
            out = out + v[:, 128 * q : 128 * q + 128]
        return out

    def forward(t):
        cols = tile(t)
        pre_s[...] = jnp.dot(joined[...], W[:, cols], preferred_element_type=f32)

        def common(ch):
            sv = score_ref[:, cols]
            pre = pre_s[ch, :]
            sig = 1.0 / (1.0 + jnp.exp(-pre))
            gate_s[ch, :] += lanes(pre * sig * sv)
            sl = sig * (1.0 + pre * (1.0 - sig)) * sv
            slope_s[ch, cols] = sl
            return sv, pre, sig, sl

        @pl.loop(0, toks // CHUNK)
        def _(u):
            common(pl.ds(pl.multiple_of(u * CHUNK, CHUNK), CHUNK))

        @pl.loop(0, toks // CHUNK)
        def _(u):
            ch = pl.ds(pl.multiple_of(u * CHUNK, CHUNK), CHUNK)
            sv, pre, sig, sl = common(pl.ds(pl.multiple_of(toks + u * CHUNK, CHUNK), CHUNK))
            R[pl.ds(pl.multiple_of(lift + u * CHUNK, CHUNK), CHUNK), cols] = sl.astype(bf16)
            curve_s[ch, cols] = sig * (1.0 - sig) * (2.0 + pre * (1.0 - 2.0 * sig)) * sv

        made = R.at[lift : lift + toks, cols]
        send(made, R.at[lift_p : lift_p + toks, cols], R_s.at[1, t], R_r.at[1, t], partner)
        liftT[...] = made[...].T

        @pl.loop(0, W.shape[0] // TILE)
        def _(u):
            ch = pl.ds(pl.multiple_of(u * TILE, TILE), TILE)
            igT[ch, :] += jnp.dot(W[ch, cols], liftT[...], preferred_element_type=f32)

    stage_a(0)
    for b in range(n_z):
        send(
            tokT.at[rblk(2 * hop(b) + 1 - c), :], L.at[b, :, 2 * toks : 4 * toks],
            tok_s.at[b], tok_r.at[b], partner, True,
        )
        L[b, :, 0 : 2 * toks] = tokT[rblk(2 * hop(b) + c), :]
    stage_b(0)

    @pl.loop(0, n_tiles)
    def _(t):
        @pl.when(t + 1 < n_tiles)
        def _():
            stage_a(t + 1)

        stage_c(t)
        stage_d(t)
        forward(t)

        @pl.when(t + 1 < n_tiles)
        def _():
            stage_b(t + 1)

    @pl.loop(0, W.shape[0] // TILE)
    def _(t):
        cols = pl.ds(pl.multiple_of(t * TILE, TILE), TILE)
        r = (loss_scale * R1_WEIGHT * igT[cols, :]).astype(bf16)
        r1T[cols, 0:toks] = r
        r1[:, cols] = r.T

    for b in range(n_z):
        send(
            r1T.at[rblk(2 * hop(b) + 1 - c), :], L.at[b, :, lift_p : lift_p + pad],
            r1_s.at[b], r1_r.at[b], partner, True,
        )
        L[b, :, lift:lift_p] = r1T[rblk(2 * hop(b) + c), :]

    gate = jnp.sum(gate_s[...], axis=1, keepdims=True)
    gate_s[0:toks, :] = jnp.broadcast_to(loss_scale / (1.0 + jnp.exp(-gate[:toks])), (toks, 128))
    gate_s[toks : 2 * toks, :] = jnp.broadcast_to(-loss_scale / (1.0 + jnp.exp(gate[toks:])), (toks, 128))

    def gated(ch, cols):
        return jnp.concatenate([gate_s[ch, :]] * (TILE // 128), 1) * slope_s[ch, cols]

    @pl.loop(0, n_tiles)
    def _(t):
        cols = tile(t)
        pre_s[0:toks, :] = jnp.dot(r1[...], W[:, cols], preferred_element_type=f32)

        @pl.loop(0, toks // CHUNK)
        def _(u):
            ch = pl.ds(pl.multiple_of(u * CHUNK, CHUNK), CHUNK)
            R[ch, cols] = gated(ch, cols).astype(bf16)
            low = pl.ds(pl.multiple_of(toks + u * CHUNK, CHUNK), CHUNK)
            R[low, cols] = (gated(low, cols) + pre_s[ch, :] * curve_s[ch, cols]).astype(bf16)

        send(R.at[0 : 2 * toks, cols], R.at[2 * toks : 4 * toks, cols], R_s.at[0, t], R_r.at[0, t], partner)

    for b in range(n_z):
        arrived(L.at[b, :, 2 * toks : 4 * toks], tok_r.at[b])
        arrived(L.at[b, :, lift_p : lift_p + pad], r1_r.at[b])
    @pl.loop(0, n_tiles)
    def _(t):
        arrived(R.at[lift_p : lift_p + toks, tile(t)], R_r.at[1, t])
        arrived(R.at[2 * toks : 4 * toks, tile(t)], R_r.at[0, t])

    last = n_z - 1

    def products(p):
        two = pl.ds(2 * p, 2)

        @pl.loop(0, n_tiles)
        def _(t):
            cols = tile(t)
            left = L[two].reshape(2 * rows, L.shape[2])
            G[two, :, cols] = jnp.dot(left, R[:, cols], preferred_element_type=f32).reshape(2, rows, TILE)

    def far_rows(k):
        @pl.loop(0, n_tiles)
        def _(t):
            for u in range(0, zrow, CHUNK):
                ez[k, t, u : u + CHUNK, :] = encode(G[k, xr + u : xr + u + CHUNK, tile(t)])

        send(ez.at[k], zf.at[k], zf_s.at[k], zf_r.at[k], to_z(hop(k)))

    def over(m, body):
        @pl.loop(0, m // CHUNK, unroll=True)
        def _(u):
            body(pl.multiple_of(u * CHUNK, CHUNK))

    def at(start):
        return pl.ds(pl.multiple_of(start, CHUNK), CHUNK)

    def spans(own):
        if not own:
            return 0, xr + zrow, xr
        return 0, hr, hr

    def step1(k, own=False):
        bx, by, m = spans(own)
        if own:
            for i in range(last):
                arrived(zf.at[i], zf_r.at[i])

            @pl.loop(0, n_tiles)
            def _(t):
                for u in range(0, zrow, CHUNK):
                    mid = G[k, xr + u : xr + u + CHUNK, tile(t)]
                    for i in range(last):
                        mid = mid + decode(zf[i, t, u : u + CHUNK, :])
                    G[k, xr + u : xr + u + CHUNK, tile(t)] = mid
        for j in range(2):
            def put_x(r):
                ex1[k, j, at(r), :] = encode(G[k, at(bx + r), quarter(2 * j + 1 - x)])

            over(m, put_x)
            part = pl.ds(0, m)
            send(ex1.at[k, j, part], rx1.at[k, j, part], g_s.at[k, j], g_r.at[k, j], to_x)

            def put_y(r):
                ey1[k, j, at(r), :] = encode(G[k, at(by + r), quarter(2 * (1 - y) + j)])

            over(m, put_y)
            send(ey1.at[k, j, part], ry1.at[k, j, part], g_s.at[k, 2 + j], g_r.at[k, 2 + j], to_y)

    def step2(k, own=False):
        bx, by, m = spans(own)
        part = pl.ds(0, m)
        for j in range(2):
            arrived(rx1.at[k, j, part], g_r.at[k, j])
            arrived(ry1.at[k, j, part], g_r.at[k, 2 + j])

        def put_x(r):
            ex2[k, at(r), :] = encode(G[k, at(bx + r), quarter(gy)] + decode(rx1[k, 1 - y, at(r), :]))

        over(m, put_x)
        send(ex2.at[k, part], rx2.at[k, part], g_s.at[k, 4], g_r.at[k, 4], to_y)

        def put_y(r):
            ey2[k, at(r), :] = encode(G[k, at(by + r), quarter(gx)] + decode(ry1[k, 1 - x, at(r), :]))

        over(m, put_y)
        send(ey2.at[k, part], ry2.at[k, part], g_s.at[k, 5], g_r.at[k, 5], to_x)

    def step3(k, own=False):
        bx, by, m = spans(own)
        arrived(rx2.at[k, pl.ds(0, m)], g_r.at[k, 4])
        arrived(ry2.at[k, pl.ds(0, m)], g_r.at[k, 5])

        def sum_x(r):
            return G[k, at(bx + r), quarter(g)] + decode(rx1[k, y, at(r), :]) + decode(rx2[k, at(r), :])

        def sum_y(r):
            return G[k, at(by + r), quarter(g)] + decode(ry1[k, x, at(r), :]) + decode(ry2[k, at(r), :])

        if not own:
            def put(r):
                S[k, at(r), :] = encode(sum_x(r))
                S[k, at(xr + r), :] = encode(sum_y(r))

            over(m, put)
            send(S.at[k], rz.at[k], z_s.at[k], z_r.at[k], to_z(hop(k)))
        else:
            def far(r):
                out = decode(rz[0, at(r), :])
                for i in range(1, last):
                    out = out + decode(rz[i, at(r), :])
                return out

            def both(r):
                A[g, at(r), :] = encode(sum_x(r) + far(r))
                A[g, at(xr + zrow + r), :] = encode(sum_y(xr + zrow - hr + r) + far(xr + r))

            def only(r):
                A[g, at(xr + r), :] = encode(sum_x(xr + r))
                A[g, at(hr + r), :] = encode(sum_y(r))

            over(xr, both)
            over(zrow // 2, only)

    def unpack(j):
        def put(r):
            out_ref[at(r), quarter(j)] = decode(A[j, at(r), :])

        over(rows, put)

    @pl.loop(0, last)
    def _(k):
        @pl.when(k % 2 == 0)
        def _():
            products(k // 2)

        far_rows(k)
        step1(k)

    @pl.loop(0, last - 1)
    def _(k):
        step2(k)

    step1(last, True)

    @pl.loop(0, last)
    def _(k):
        @pl.when(k == 1)
        def _():
            step2(last - 1)

        step3(k)

    step2(last, True)
    for k in range(last):
        arrived(rz.at[k], z_r.at[k])
    step3(last, True)
    send(A.at[g], A.at[g], a_s.at[0], a_r.at[0], to_x, True)
    send(A.at[g], A.at[g], a_s.at[1], a_r.at[1], to_y, True)
    unpack(g)
    lo, hi = pl.ds(0, hr), pl.ds(hr, hr)
    arrived(A.at[gx], a_r.at[0])
    send(A.at[gx, lo], A.at[gx, lo], a_s.at[2], a_r.at[2], to_y, True)
    arrived(A.at[gy], a_r.at[1])
    send(A.at[gy, hi], A.at[gy, hi], a_s.at[3], a_r.at[3], to_x, True)
    unpack(gx)
    unpack(gy)
    arrived(A.at[gd, lo], a_r.at[2])
    arrived(A.at[gd, hi], a_r.at[3])
    unpack(gd)
    for cp in pending:
        cp.wait_send()

    @pl.loop(0, n_tiles)
    def _(t):
        for i in order:
            for m in range(3):
                sent(W.at[0:rows, 0:sub], w_s.at[t, i, m])
            for m in range(3, 5):
                sent(W.at[0:hr, 0:sub], w_s.at[t, i, m])
        for i in range(n_z):
            sent(W.at[0:rows, 0:TILE], wp_s.at[t, i])
        sent(R.at[0:toks, tile(t)], R_s.at[1, t])
        sent(R.at[0 : 2 * toks, tile(t)], R_s.at[0, t])

    def drain(k, own=False):
        part = pl.ds(0, spans(own)[2])
        for j in range(2):
            sent(ex1.at[k, j, part], g_s.at[k, j])
            sent(ey1.at[k, j, part], g_s.at[k, 2 + j])
        sent(ex2.at[k, part], g_s.at[k, 4])
        sent(ey2.at[k, part], g_s.at[k, 5])
        if not own:
            sent(ez.at[k], zf_s.at[k])
            sent(S.at[k], z_s.at[k])

    @pl.loop(0, last)
    def _(k):
        drain(k)

    drain(last, True)


def fused(n_z, loss_scale, fake_tokens, real_tokens, proj_weight, score_vector):
    toks, d_in = fake_tokens.shape[1:]
    rows, hid = proj_weight.shape
    f32, bf16 = jnp.float32, jnp.bfloat16
    vm, dma = pltpu.VMEM, pltpu.SemaphoreType.DMA
    tiles = hid // TILE
    pad = -(-toks // 128) * 128
    hr = rows // 2
    zrow = rows // 6
    xr = hr - zrow // 2
    scratch = [
        vm((d_in, hid), bf16),
        vm((2 * toks, d_in), bf16),
        vm((d_in, 2 * toks), bf16),
        vm((n_z, rows, 4 * toks + 2 * pad), bf16),
        vm((d_in, toks), f32),
        vm((TILE, toks), bf16),
        vm((toks, d_in), bf16),
        vm((d_in, pad), bf16),
        vm((4 * toks + 2 * pad, hid), bf16),
        vm((2 * toks, TILE), f32),
        vm((2 * toks, hid), f32),
        vm((toks, hid), f32),
        vm((2 * toks, 128), f32),
        vm((n_z, rows, hid), f32),
        vm((n_z, 2, hr, CODED), bf16),
        vm((n_z, 2, hr, CODED), bf16),
        vm((n_z, hr, CODED), bf16),
        vm((n_z, hr, CODED), bf16),
        vm((n_z, 2, hr, CODED), bf16),
        vm((n_z, 2, hr, CODED), bf16),
        vm((n_z, hr, CODED), bf16),
        vm((n_z, hr, CODED), bf16),
        vm((n_z - 1, 2 * xr, CODED), bf16),
        vm((n_z - 1, 2 * xr, CODED), bf16),
        vm((n_z - 1, tiles, zrow, CODED), bf16),
        vm((n_z - 1, tiles, zrow, CODED), bf16),
        vm((4, rows, CODED), bf16),
        dma((tiles, n_z - 1, 5)), dma((tiles, n_z - 1, 5)),
        dma((tiles, n_z)), dma((tiles, n_z)),
        dma((n_z,)), dma((n_z,)),
        dma((n_z,)), dma((n_z,)),
        dma((2, tiles)), dma((2, tiles)),
        dma((n_z, 6)), dma((n_z, 6)),
        dma((n_z - 1,)), dma((n_z - 1,)),
        dma((n_z - 1,)), dma((n_z - 1,)),
        dma((4,)), dma((4,)),
    ]
    return pl.pallas_call(
        functools.partial(kernel, n_z, loss_scale),
        out_shape=jax.ShapeDtypeStruct((rows, hid), f32),
        in_specs=[pl.BlockSpec(memory_space=pltpu.VMEM)] * 4,
        out_specs=pl.BlockSpec(memory_space=pltpu.VMEM),
        scratch_shapes=scratch,
        compiler_params=pltpu.CompilerParams(
            collective_id=0, has_side_effects=True, vmem_limit_bytes=58 * 1024 * 1024
        ),
    )(fake_tokens[0], real_tokens[0], proj_weight, score_vector[None, :])


def solution(mesh):
    in_specs = (P("grp", "seq", None), P("grp", "seq", None), P("seq", None), P())
    out_specs = P("seq", None)
    n_grp, n_seq = mesh.shape["grp"], mesh.shape["seq"]

    def body(fake_tokens, real_tokens, proj_weight, score_vector):
        toks = fake_tokens.shape[1]
        rows, hid = proj_weight.shape
        fits = n_grp == 4 and n_seq == 8 and hid == 4 * TILE and rows % 192 == 0 and toks % 64 == 0
        if not fits:
            return per_device(fake_tokens, real_tokens, proj_weight, score_vector)
        loss_scale = math.sqrt(hid / (n_grp * n_seq * toks))
        return fused(n_seq // 2, loss_scale, fake_tokens, real_tokens, proj_weight, score_vector)

    return jax.shard_map(body, mesh=mesh, in_specs=in_specs, out_specs=out_specs, check_vma=False)
```

```python
import functools
import math

import jax
import jax.numpy as jnp
from jax import lax
from jax.experimental import pallas as pl
from jax.experimental.pallas import tpu as pltpu
from jax.sharding import PartitionSpec as P

R1_WEIGHT = 40.0
MESH = pl.DeviceIdType.MESH
TILE = 512
CHUNK = 16
CODED = TILE + TILE // 2
LEVELS = 21
STEPS = 2560.0


def per_device(fake_tokens, real_tokens, proj_weight, score_vector):
    fake_rows = fake_tokens[0]
    real_rows = real_tokens[0]
    tok_count = fake_rows.shape[0]
    hid_width = proj_weight.shape[1]
    loss_scale = math.sqrt(hid_width / (lax.axis_size("grp") * lax.axis_size("seq") * tok_count))
    joined = jnp.concatenate([fake_rows, real_rows], 0)
    full_weight = lax.all_gather(proj_weight, "seq", axis=0, tiled=True)
    preact = jnp.dot(joined, full_weight, preferred_element_type=jnp.float32)
    squash = jax.nn.sigmoid(preact)
    slopes = squash * (1.0 + preact * (1.0 - squash))
    curves = squash * (1.0 - squash) * (2.0 + preact * (1.0 - 2.0 * squash))
    logits = jnp.dot(preact * squash, score_vector, precision=lax.Precision.HIGHEST)
    slopes_real = slopes[tok_count:]
    lifted = (slopes_real * score_vector).astype(jnp.bfloat16)
    input_grad = lax.dot_general(
        lifted, full_weight, (((1,), (1,)), ((), ())), preferred_element_type=jnp.float32
    )
    r1_cot = (loss_scale * R1_WEIGHT * input_grad).astype(jnp.bfloat16)
    back_grad = jnp.dot(r1_cot, full_weight, preferred_element_type=jnp.float32)
    fake_cot = (
        loss_scale * jax.nn.sigmoid(logits[:tok_count])[:, None] * slopes[:tok_count] * score_vector
    ).astype(jnp.bfloat16)
    real_cot = (
        -loss_scale * jax.nn.sigmoid(-logits[tok_count:])[:, None] * slopes_real * score_vector
        + back_grad * score_vector * curves[tok_count:]
    ).astype(jnp.bfloat16)
    left_rows = jnp.concatenate([fake_rows, real_rows, r1_cot], 0)
    right_rows = jnp.concatenate([fake_cot, real_cot, lifted], 0)
    grad_term = lax.dot_general(
        left_rows, right_rows, (((0,), (0,)), ((), ())), preferred_element_type=jnp.float32
    )
    grad_shard = lax.psum_scatter(grad_term, "seq", scatter_dimension=0, tiled=True)
    return lax.psum(grad_shard, "grp")


def encode(v):
    head = v.astype(jnp.bfloat16)
    wide = head.astype(jnp.float32)
    scale = pl.reciprocal(jnp.maximum(jnp.abs(wide), 1e-30), approx=True) * STEPS
    q = jnp.round((v - wide) * scale)
    n = v.shape[1] // 2
    return jnp.concatenate([head, (q[:, :n] * LEVELS + q[:, n:]).astype(jnp.bfloat16)], 1)


def decode(e):
    n = e.shape[1] // 3
    wide = e[:, : 2 * n].astype(jnp.float32)
    word = e[:, 2 * n :].astype(jnp.float32)
    first = jnp.round(word * (1.0 / LEVELS))
    q = jnp.concatenate([first, word - LEVELS * first], 1)
    return wide + jnp.abs(wide) * (q * (1.0 / STEPS))


def kernel(
    n_z, loss_scale,
    fake_ref, real_ref, w_ref, score_ref, out_ref,
    W, joined, tokT, tokP, igT, liftT, r1, r1T, r1P, R, RP, pre_s, slope_s, curve_s, gate_s,
    G, ex1, ey1, ex2, ey2, rx1, ry1, rx2, ry2, S, rz, ez, zf, A,
    w_s, w_r, wp_s, wp_r, tok_s, tok_r, r1_s, r1_r, R_s, R_r, g_s, g_r, z_s, z_r, zf_s, zf_r, a_s, a_r,
):
    f32 = jnp.float32
    bf16 = jnp.bfloat16
    rows, hid = w_ref.shape
    toks = fake_ref.shape[0]
    n_tiles = hid // TILE
    sub = rows // 4
    cut = sub // 48 * 16 if sub % 48 == 0 else sub // 32 * 16
    hr = rows // 2
    zrow = zf.shape[2]
    xr = hr - zrow // 2
    g = lax.axis_index("grp")
    s = lax.axis_index("seq")
    y, x = g // 2, g % 2
    z, c = s // 2, s % 2
    gx, gy, gd = 2 * y + 1 - x, 2 * (1 - y) + x, 3 - g
    to_x = {"grp": gx, "seq": s}
    to_y = {"grp": gy, "seq": s}
    partner = {"grp": g, "seq": 2 * z + 1 - c}

    def to_z(zt):
        return {"grp": g, "seq": 2 * zt + c}

    barrier = pltpu.get_barrier_semaphore()
    greet = [to_x, to_y, partner] + [to_z((z + d) % n_z) for d in range(1, n_z)]
    for dev in greet:
        pl.semaphore_signal(barrier, inc=1, device_id=dev, device_id_type=MESH)
    pl.semaphore_wait(barrier, len(greet))

    pending = []

    def send(src, dst, ssem, rsem, dev, keep=False):
        cp = pltpu.make_async_remote_copy(
            src_ref=src, dst_ref=dst, send_sem=ssem, recv_sem=rsem, device_id=dev, device_id_type=MESH
        )
        cp.start()
        if keep:
            pending.append(cp)

    def arrived(ref, rsem):
        pltpu.make_async_remote_copy(
            src_ref=ref, dst_ref=ref, send_sem=rsem, recv_sem=rsem, device_id=partner, device_id_type=MESH
        ).wait_recv()

    def sent(ref, ssem):
        pltpu.make_async_remote_copy(
            src_ref=ref, dst_ref=ref, send_sem=ssem, recv_sem=ssem, device_id=partner, device_id_type=MESH
        ).wait_send()

    def rblk(seq):
        return pl.ds(pl.multiple_of(rows * seq, 16), rows)

    def quarter(j):
        return pl.ds(pl.multiple_of(j * TILE, TILE), TILE)

    def part_of(seq, j):
        return pl.ds(pl.multiple_of(rows * seq + sub * j, 16), sub)

    def cut_of(seq, j, i, h):
        first = cut if i % 2 == 0 else sub - cut
        size = first if h == 0 else sub - first
        return pl.ds(pl.multiple_of(rows * seq + sub * j + h * first, 16), size)

    def tile(t):
        return pl.ds(pl.multiple_of(t * TILE, TILE), TILE)

    order = [0, 2, 1] if n_z == 4 else list(range(n_z - 1))
    @pl.loop(0, n_tiles)
    def _(t):
        for i in order:
            mine = pl.ds(pl.multiple_of(sub * g, 16), sub)
            send(
                w_ref.at[mine, tile(t)], W.at[t, part_of(s, g), :], w_s.at[t, i, 0], w_r.at[t, i, 0],
                to_z((z + 1 + i) % n_z),
            )
        send(w_ref.at[:, tile(t)], W.at[t, rblk(s), :], wp_s.at[t, n_z - 1], wp_r.at[t, n_z - 1], partner)
    for t in range(n_tiles):
        W[t, rblk(s), :] = w_ref[:, t * TILE : (t + 1) * TILE]
    joined[0:toks, :] = fake_ref[...]
    joined[toks : 2 * toks, :] = real_ref[...]
    igT[...] = jnp.zeros_like(igT)
    gate_s[...] = jnp.zeros_like(gate_s)

    @pl.loop(0, joined.shape[1] // TILE)
    def _(t):
        cols = pl.ds(pl.multiple_of(t * TILE, TILE), TILE)
        tokT[cols, :] = joined[:, cols].T

    def zseq(i, parity):
        return 2 * ((z + n_z - 1 - i) % n_z) + parity

    def stage_a(t):
        for i in order:
            mine = W.at[t, part_of(zseq(i, c), g), :]
            arrived(mine, w_r.at[t, i, 0])
            send(mine, mine, w_s.at[t, i, 1], w_r.at[t, i, 1], to_x)
            send(mine, mine, w_s.at[t, i, 2], w_r.at[t, i, 2], to_y)

    def stage_b(t):
        for i in order:
            sq = zseq(i, c)
            ref = W.at[t, part_of(sq, gx), :]
            arrived(ref, w_r.at[t, i, 1])
            h = W.at[t, cut_of(sq, gx, i, 0), :]
            send(h, h, w_s.at[t, i, 3], w_r.at[t, i, 3], to_y)
            ref = W.at[t, part_of(sq, gy), :]
            arrived(ref, w_r.at[t, i, 2])
            h = W.at[t, cut_of(sq, gy, i, 1), :]
            send(h, h, w_s.at[t, i, 4], w_r.at[t, i, 4], to_x)

    def stage_c(t):
        for i in order:
            sq = zseq(i, c)
            arrived(W.at[t, cut_of(sq, gd, i, 0), :], w_r.at[t, i, 3])
            arrived(W.at[t, cut_of(sq, gd, i, 1), :], w_r.at[t, i, 4])
            ref = W.at[t, rblk(sq), :]
            send(ref, ref, wp_s.at[t, i], wp_r.at[t, i], partner)

    def stage_d(t):
        arrived(W.at[t, rblk(2 * z + 1 - c), :], wp_r.at[t, n_z - 1])
        for i in order:
            arrived(W.at[t, rblk(zseq(i, 1 - c)), :], wp_r.at[t, i])

    def lanes(v):
        out = v[:, 0:128]
        for q in range(1, TILE // 128):
            out = out + v[:, 128 * q : 128 * q + 128]
        return out

    def forward(t):
        cols = tile(t)
        pre_s[...] = jnp.dot(joined[...], W[t], preferred_element_type=f32)

        def common(ch):
            sv = score_ref[:, cols]
            pre = pre_s[ch, :]
            sig = 1.0 / (1.0 + jnp.exp(-pre))
            gate_s[ch, :] += lanes(pre * sig * sv)
            sl = sig * (1.0 + pre * (1.0 - sig)) * sv
            slope_s[ch, cols] = sl
            return sv, pre, sig, sl

        @pl.loop(0, toks // CHUNK)
        def _(u):
            common(pl.ds(pl.multiple_of(u * CHUNK, CHUNK), CHUNK))

        @pl.loop(0, toks // CHUNK)
        def _(u):
            ch = pl.ds(pl.multiple_of(u * CHUNK, CHUNK), CHUNK)
            sv, pre, sig, sl = common(pl.ds(pl.multiple_of(toks + u * CHUNK, CHUNK), CHUNK))
            R[2, ch, cols] = sl.astype(bf16)
            curve_s[ch, cols] = sig * (1.0 - sig) * (2.0 + pre * (1.0 - 2.0 * sig)) * sv

        send(R.at[2, :, cols], RP.at[2, :, cols], R_s.at[2, t], R_r.at[2, t], partner)
        liftT[...] = R[2, :, cols].T

        @pl.loop(0, W.shape[1] // TILE)
        def _(u):
            ch = pl.ds(pl.multiple_of(u * TILE, TILE), TILE)
            igT[ch, :] += jnp.dot(W[t, ch, :], liftT[...], preferred_element_type=f32)

    stage_a(0)
    for b in range(n_z):
        send(tokT.at[rblk(2 * b + 1 - c), :], tokP.at[b], tok_s.at[b], tok_r.at[b], partner, True)
    stage_b(0)

    @pl.loop(0, n_tiles)
    def _(t):
        @pl.when(t + 1 < n_tiles)
        def _():
            stage_a(t + 1)

        stage_c(t)
        stage_d(t)
        forward(t)

        @pl.when(t + 1 < n_tiles)
        def _():
            stage_b(t + 1)

    @pl.loop(0, W.shape[1] // TILE)
    def _(t):
        cols = pl.ds(pl.multiple_of(t * TILE, TILE), TILE)
        r = (loss_scale * R1_WEIGHT * igT[cols, :]).astype(bf16)
        r1T[cols, :] = r
        r1[:, cols] = r.T

    for b in range(n_z):
        send(r1T.at[rblk(2 * b + 1 - c), :], r1P.at[b], r1_s.at[b], r1_r.at[b], partner, True)

    gate = jnp.sum(gate_s[...], axis=1, keepdims=True)
    gate_s[0:toks, :] = jnp.broadcast_to(loss_scale / (1.0 + jnp.exp(-gate[:toks])), (toks, 128))
    gate_s[toks : 2 * toks, :] = jnp.broadcast_to(-loss_scale / (1.0 + jnp.exp(gate[toks:])), (toks, 128))

    def gated(ch, cols):
        return jnp.concatenate([gate_s[ch, :]] * (TILE // 128), 1) * slope_s[ch, cols]

    @pl.loop(0, n_tiles)
    def _(t):
        cols = tile(t)
        pre_s[0:toks, :] = jnp.dot(r1[...], W[t], preferred_element_type=f32)

        @pl.loop(0, toks // CHUNK)
        def _(u):
            ch = pl.ds(pl.multiple_of(u * CHUNK, CHUNK), CHUNK)
            R[0, ch, cols] = gated(ch, cols).astype(bf16)
            low = pl.ds(pl.multiple_of(toks + u * CHUNK, CHUNK), CHUNK)
            R[1, ch, cols] = (gated(low, cols) + pre_s[ch, :] * curve_s[ch, cols]).astype(bf16)

        send(R.at[0:2, :, cols], RP.at[0:2, :, cols], R_s.at[0, t], R_r.at[0, t], partner)

    for b in range(n_z):
        arrived(tokP.at[b], tok_r.at[b])
        arrived(r1P.at[b], r1_r.at[b])
    @pl.loop(0, n_tiles)
    def _(t):
        arrived(RP.at[2, :, tile(t)], R_r.at[2, t])
        arrived(RP.at[0:2, :, tile(t)], R_r.at[0, t])

    last = n_z - 1

    def hop(k):
        return (z + 1 + k) % n_z

    def block(k, own=False):
        zb = hop(k)
        mine = rblk(2 * zb + c)

        @pl.loop(0, n_tiles)
        def _(t):
            cols = pl.ds(pl.multiple_of(t * TILE, TILE), TILE)
            acc = jnp.dot(tokT[mine, :], R[0:2, :, cols].reshape(2 * toks, TILE), preferred_element_type=f32)
            acc += jnp.dot(r1T[mine, :], R[2, :, cols], preferred_element_type=f32)
            acc += jnp.dot(tokP[zb], RP[0:2, :, cols].reshape(2 * toks, TILE), preferred_element_type=f32)
            acc += jnp.dot(r1P[zb], RP[2, :, cols], preferred_element_type=f32)
            G[k, :, cols] = acc

        if not own:
            @pl.loop(0, n_tiles)
            def _(t):
                for u in range(0, zrow, CHUNK):
                    ez[k, t, u : u + CHUNK, :] = encode(G[k, xr + u : xr + u + CHUNK, tile(t)])

            send(ez.at[k], zf.at[k], zf_s.at[k], zf_r.at[k], to_z(zb))

    def over(m, body):
        @pl.loop(0, m // CHUNK)
        def _(u):
            body(pl.multiple_of(u * CHUNK, CHUNK))

    def at(start):
        return pl.ds(pl.multiple_of(start, CHUNK), CHUNK)

    def spans(own):
        if not own:
            return 0, xr + zrow, xr
        return 0, hr, hr

    def step1(k, own=False):
        bx, by, m = spans(own)
        if own:
            for i in range(last):
                arrived(zf.at[i], zf_r.at[i])

            @pl.loop(0, n_tiles)
            def _(t):
                for u in range(0, zrow, CHUNK):
                    mid = G[k, xr + u : xr + u + CHUNK, tile(t)]
                    for i in range(last):
                        mid = mid + decode(zf[i, t, u : u + CHUNK, :])
                    G[k, xr + u : xr + u + CHUNK, tile(t)] = mid
        for j in range(2):
            def put_x(r):
                ex1[k, j, at(r), :] = encode(G[k, at(bx + r), quarter(2 * j + 1 - x)])

            over(m, put_x)
            part = pl.ds(0, m)
            send(ex1.at[k, j, part], rx1.at[k, j, part], g_s.at[k, j], g_r.at[k, j], to_x)

            def put_y(r):
                ey1[k, j, at(r), :] = encode(G[k, at(by + r), quarter(2 * (1 - y) + j)])

            over(m, put_y)
            send(ey1.at[k, j, part], ry1.at[k, j, part], g_s.at[k, 2 + j], g_r.at[k, 2 + j], to_y)

    def step2(k, own=False):
        bx, by, m = spans(own)
        part = pl.ds(0, m)
        for j in range(2):
            arrived(rx1.at[k, j, part], g_r.at[k, j])
            arrived(ry1.at[k, j, part], g_r.at[k, 2 + j])

        def put_x(r):
            ex2[k, at(r), :] = encode(G[k, at(bx + r), quarter(gy)] + decode(rx1[k, 1 - y, at(r), :]))

        over(m, put_x)
        send(ex2.at[k, part], rx2.at[k, part], g_s.at[k, 4], g_r.at[k, 4], to_y)

        def put_y(r):
            ey2[k, at(r), :] = encode(G[k, at(by + r), quarter(gx)] + decode(ry1[k, 1 - x, at(r), :]))

        over(m, put_y)
        send(ey2.at[k, part], ry2.at[k, part], g_s.at[k, 5], g_r.at[k, 5], to_x)

    def step3(k, own=False):
        bx, by, m = spans(own)
        arrived(rx2.at[k, pl.ds(0, m)], g_r.at[k, 4])
        arrived(ry2.at[k, pl.ds(0, m)], g_r.at[k, 5])

        def sum_x(r):
            return G[k, at(bx + r), quarter(g)] + decode(rx1[k, y, at(r), :]) + decode(rx2[k, at(r), :])

        def sum_y(r):
            return G[k, at(by + r), quarter(g)] + decode(ry1[k, x, at(r), :]) + decode(ry2[k, at(r), :])

        if not own:
            def put(r):
                S[k, at(r), :] = encode(sum_x(r))
                S[k, at(xr + r), :] = encode(sum_y(r))

            over(m, put)
            send(S.at[k], rz.at[k], z_s.at[k], z_r.at[k], to_z(hop(k)))
        else:
            def far(r):
                out = decode(rz[0, at(r), :])
                for i in range(1, last):
                    out = out + decode(rz[i, at(r), :])
                return out

            def both(r):
                A[g, at(r), :] = encode(sum_x(r) + far(r))
                A[g, at(xr + zrow + r), :] = encode(sum_y(xr + zrow - hr + r) + far(xr + r))

            def only(r):
                A[g, at(xr + r), :] = encode(sum_x(xr + r))
                A[g, at(hr + r), :] = encode(sum_y(r))

            over(xr, both)
            over(zrow // 2, only)

    def unpack(j):
        def put(r):
            out_ref[at(r), quarter(j)] = decode(A[j, at(r), :])

        over(rows, put)

    @pl.loop(0, last)
    def _(k):
        block(k)
        step1(k)

        @pl.when(k >= 1)
        def _():
            step2(k - 1)

    block(last, True)
    step1(last, True)

    @pl.loop(0, last)
    def _(k):
        @pl.when(k == 1)
        def _():
            step2(last - 1)

        step3(k)

    step2(last, True)
    for k in range(last):
        arrived(rz.at[k], z_r.at[k])
    step3(last, True)
    send(A.at[g], A.at[g], a_s.at[0], a_r.at[0], to_x, True)
    send(A.at[g], A.at[g], a_s.at[1], a_r.at[1], to_y, True)
    unpack(g)
    lo, hi = pl.ds(0, hr), pl.ds(hr, hr)
    arrived(A.at[gx], a_r.at[0])
    send(A.at[gx, lo], A.at[gx, lo], a_s.at[2], a_r.at[2], to_y, True)
    arrived(A.at[gy], a_r.at[1])
    send(A.at[gy, hi], A.at[gy, hi], a_s.at[3], a_r.at[3], to_x, True)
    unpack(gx)
    unpack(gy)
    arrived(A.at[gd, lo], a_r.at[2])
    arrived(A.at[gd, hi], a_r.at[3])
    unpack(gd)
    for cp in pending:
        cp.wait_send()

    @pl.loop(0, n_tiles)
    def _(t):
        for i in order:
            for m in range(3):
                sent(W.at[t, 0:sub, :], w_s.at[t, i, m])
            for h in range(2):
                sent(W.at[t, cut_of(0, 0, i, h), :], w_s.at[t, i, 3 + h])
        for i in range(n_z):
            sent(W.at[t, 0:rows, :], wp_s.at[t, i])
        sent(R.at[2, :, tile(t)], R_s.at[2, t])
        sent(R.at[0:2, :, tile(t)], R_s.at[0, t])

    def drain(k, own=False):
        part = pl.ds(0, spans(own)[2])
        for j in range(2):
            sent(ex1.at[k, j, part], g_s.at[k, j])
            sent(ey1.at[k, j, part], g_s.at[k, 2 + j])
        sent(ex2.at[k, part], g_s.at[k, 4])
        sent(ey2.at[k, part], g_s.at[k, 5])
        if not own:
            sent(ez.at[k], zf_s.at[k])
            sent(S.at[k], z_s.at[k])

    @pl.loop(0, last)
    def _(k):
        drain(k)

    drain(last, True)


def fused(n_z, loss_scale, fake_tokens, real_tokens, proj_weight, score_vector):
    toks, d_in = fake_tokens.shape[1:]
    rows, hid = proj_weight.shape
    f32, bf16 = jnp.float32, jnp.bfloat16
    vm, dma = pltpu.VMEM, pltpu.SemaphoreType.DMA
    tiles = hid // TILE
    hr = rows // 2
    zrow = rows // 6
    xr = hr - zrow // 2
    scratch = [
        vm((tiles, d_in, TILE), bf16),
        vm((2 * toks, d_in), bf16),
        vm((d_in, 2 * toks), bf16),
        vm((n_z, rows, 2 * toks), bf16),
        vm((d_in, toks), f32),
        vm((TILE, toks), bf16),
        vm((toks, d_in), bf16),
        vm((d_in, toks), bf16),
        vm((n_z, rows, toks), bf16),
        vm((3, toks, hid), bf16),
        vm((3, toks, hid), bf16),
        vm((2 * toks, TILE), f32),
        vm((2 * toks, hid), f32),
        vm((toks, hid), f32),
        vm((2 * toks, 128), f32),
        vm((n_z, rows, hid), f32),
        vm((n_z, 2, hr, CODED), bf16),
        vm((n_z, 2, hr, CODED), bf16),
        vm((n_z, hr, CODED), bf16),
        vm((n_z, hr, CODED), bf16),
        vm((n_z, 2, hr, CODED), bf16),
        vm((n_z, 2, hr, CODED), bf16),
        vm((n_z, hr, CODED), bf16),
        vm((n_z, hr, CODED), bf16),
        vm((n_z - 1, 2 * xr, CODED), bf16),
        vm((n_z - 1, 2 * xr, CODED), bf16),
        vm((n_z - 1, tiles, zrow, CODED), bf16),
        vm((n_z - 1, tiles, zrow, CODED), bf16),
        vm((4, rows, CODED), bf16),
        dma((tiles, n_z - 1, 5)), dma((tiles, n_z - 1, 5)),
        dma((tiles, n_z)), dma((tiles, n_z)),
        dma((n_z,)), dma((n_z,)),
        dma((n_z,)), dma((n_z,)),
        dma((3, tiles)), dma((3, tiles)),
        dma((n_z, 6)), dma((n_z, 6)),
        dma((n_z - 1,)), dma((n_z - 1,)),
        dma((n_z - 1,)), dma((n_z - 1,)),
        dma((4,)), dma((4,)),
    ]
    return pl.pallas_call(
        functools.partial(kernel, n_z, loss_scale),
        out_shape=jax.ShapeDtypeStruct((rows, hid), f32),
        in_specs=[pl.BlockSpec(memory_space=pltpu.VMEM)] * 4,
        out_specs=pl.BlockSpec(memory_space=pltpu.VMEM),
        scratch_shapes=scratch,
        compiler_params=pltpu.CompilerParams(
            collective_id=0, has_side_effects=True, vmem_limit_bytes=58 * 1024 * 1024
        ),
    )(fake_tokens[0], real_tokens[0], proj_weight, score_vector[None, :])


def solution(mesh):
    in_specs = (P("grp", "seq", None), P("grp", "seq", None), P("seq", None), P())
    out_specs = P("seq", None)
    n_grp, n_seq = mesh.shape["grp"], mesh.shape["seq"]

    def body(fake_tokens, real_tokens, proj_weight, score_vector):
        toks = fake_tokens.shape[1]
        rows, hid = proj_weight.shape
        fits = n_grp == 4 and n_seq == 8 and hid == 4 * TILE and rows % 192 == 0 and toks % 64 == 0
        if not fits:
            return per_device(fake_tokens, real_tokens, proj_weight, score_vector)
        loss_scale = math.sqrt(hid / (n_grp * n_seq * toks))
        return fused(n_seq // 2, loss_scale, fake_tokens, real_tokens, proj_weight, score_vector)

    return jax.shard_map(body, mesh=mesh, in_specs=in_specs, out_specs=out_specs, check_vma=False)
```

```python
import functools
import math

import jax
import jax.numpy as jnp
from jax import lax
from jax.experimental import pallas as pl
from jax.experimental.pallas import tpu as pltpu
from jax.sharding import PartitionSpec as P

R1_WEIGHT = 40.0
MESH = pl.DeviceIdType.MESH
TILE = 512
CHUNK = 16
CODED = TILE + TILE // 2
LEVELS = 21
STEPS = 2560.0


def per_device(fake_tokens, real_tokens, proj_weight, score_vector):
    fake_rows = fake_tokens[0]
    real_rows = real_tokens[0]
    tok_count = fake_rows.shape[0]
    hid_width = proj_weight.shape[1]
    loss_scale = math.sqrt(hid_width / (lax.axis_size("grp") * lax.axis_size("seq") * tok_count))
    joined = jnp.concatenate([fake_rows, real_rows], 0)
    full_weight = lax.all_gather(proj_weight, "seq", axis=0, tiled=True)
    preact = jnp.dot(joined, full_weight, preferred_element_type=jnp.float32)
    squash = jax.nn.sigmoid(preact)
    slopes = squash * (1.0 + preact * (1.0 - squash))
    curves = squash * (1.0 - squash) * (2.0 + preact * (1.0 - 2.0 * squash))
    logits = jnp.dot(preact * squash, score_vector, precision=lax.Precision.HIGHEST)
    slopes_real = slopes[tok_count:]
    lifted = (slopes_real * score_vector).astype(jnp.bfloat16)
    input_grad = lax.dot_general(
        lifted, full_weight, (((1,), (1,)), ((), ())), preferred_element_type=jnp.float32
    )
    r1_cot = (loss_scale * R1_WEIGHT * input_grad).astype(jnp.bfloat16)
    back_grad = jnp.dot(r1_cot, full_weight, preferred_element_type=jnp.float32)
    fake_cot = (
        loss_scale * jax.nn.sigmoid(logits[:tok_count])[:, None] * slopes[:tok_count] * score_vector
    ).astype(jnp.bfloat16)
    real_cot = (
        -loss_scale * jax.nn.sigmoid(-logits[tok_count:])[:, None] * slopes_real * score_vector
        + back_grad * score_vector * curves[tok_count:]
    ).astype(jnp.bfloat16)
    left_rows = jnp.concatenate([fake_rows, real_rows, r1_cot], 0)
    right_rows = jnp.concatenate([fake_cot, real_cot, lifted], 0)
    grad_term = lax.dot_general(
        left_rows, right_rows, (((0,), (0,)), ((), ())), preferred_element_type=jnp.float32
    )
    grad_shard = lax.psum_scatter(grad_term, "seq", scatter_dimension=0, tiled=True)
    return lax.psum(grad_shard, "grp")


def encode(v):
    head = v.astype(jnp.bfloat16)
    wide = head.astype(jnp.float32)
    scale = pl.reciprocal(jnp.maximum(jnp.abs(wide), 1e-30), approx=True) * STEPS
    q = jnp.round((v - wide) * scale)
    n = v.shape[1] // 2
    return jnp.concatenate([head, (q[:, :n] * LEVELS + q[:, n:]).astype(jnp.bfloat16)], 1)


def decode(e):
    n = e.shape[1] // 3
    wide = e[:, : 2 * n].astype(jnp.float32)
    word = e[:, 2 * n :].astype(jnp.float32)
    first = jnp.round(word * (1.0 / LEVELS))
    q = jnp.concatenate([first, word - LEVELS * first], 1)
    return wide + jnp.abs(wide) * (q * (1.0 / STEPS))


def kernel(
    n_z, loss_scale,
    fake_ref, real_ref, w_ref, score_ref, out_ref,
    W, joined, tokT, tokP, igT, liftT, r1, r1T, r1P, R, RP, pre_s, slope_s, curve_s, gate_s,
    G, ex1, ey1, ex2, ey2, rx1, ry1, rx2, ry2, S, rz, A,
    w_s, w_r, wp_s, wp_r, tok_s, tok_r, r1_s, r1_r, R_s, R_r, g_s, g_r, z_s, z_r, a_s, a_r,
):
    f32 = jnp.float32
    bf16 = jnp.bfloat16
    rows, hid = w_ref.shape
    toks = fake_ref.shape[0]
    n_tiles = hid // TILE
    sub = TILE // 4
    hr = rows // 2
    zrow, xr = 0, hr
    g = lax.axis_index("grp")
    s = lax.axis_index("seq")
    y, x = g // 2, g % 2
    z, c = s // 2, s % 2
    gx, gy, gd = 2 * y + 1 - x, 2 * (1 - y) + x, 3 - g
    to_x = {"grp": gx, "seq": s}
    to_y = {"grp": gy, "seq": s}
    partner = {"grp": g, "seq": 2 * z + 1 - c}

    def to_z(zt):
        return {"grp": g, "seq": 2 * zt + c}

    barrier = pltpu.get_barrier_semaphore()
    greet = [to_x, to_y, partner] + [to_z((z + d) % n_z) for d in range(1, n_z)]
    for dev in greet:
        pl.semaphore_signal(barrier, inc=1, device_id=dev, device_id_type=MESH)
    pl.semaphore_wait(barrier, len(greet))

    pending = []

    def send(src, dst, ssem, rsem, dev, keep=False):
        cp = pltpu.make_async_remote_copy(
            src_ref=src, dst_ref=dst, send_sem=ssem, recv_sem=rsem, device_id=dev, device_id_type=MESH
        )
        cp.start()
        if keep:
            pending.append(cp)

    def arrived(ref, rsem):
        pltpu.make_async_remote_copy(
            src_ref=ref, dst_ref=ref, send_sem=rsem, recv_sem=rsem, device_id=partner, device_id_type=MESH
        ).wait_recv()

    def sent(ref, ssem):
        pltpu.make_async_remote_copy(
            src_ref=ref, dst_ref=ref, send_sem=ssem, recv_sem=ssem, device_id=partner, device_id_type=MESH
        ).wait_send()

    def rblk(seq):
        return pl.ds(pl.multiple_of(rows * seq, 16), rows)

    def rhalf(seq, h):
        return pl.ds(pl.multiple_of(rows * seq + hr * h, 16), hr)

    def quarter(j):
        return pl.ds(pl.multiple_of(j * TILE, TILE), TILE)

    def subq(t, j):
        return pl.ds(pl.multiple_of(t * TILE + j * sub, sub), sub)

    def tile(t):
        return pl.ds(pl.multiple_of(t * TILE, TILE), TILE)

    order = [0, 2, 1] if n_z == 4 else list(range(n_z - 1))
    @pl.loop(0, n_tiles)
    def _(t):
        for i in order:
            cols = subq(t, g)
            send(
                w_ref.at[:, cols], W.at[rblk(s), cols], w_s.at[t, i, 0], w_r.at[t, i, 0],
                to_z((z + 1 + i) % n_z),
            )
        send(w_ref.at[:, tile(t)], W.at[rblk(s), tile(t)], wp_s.at[t, n_z - 1], wp_r.at[t, n_z - 1], partner)
    W[rblk(s), :] = w_ref[...]
    joined[0:toks, :] = fake_ref[...]
    joined[toks : 2 * toks, :] = real_ref[...]
    igT[...] = jnp.zeros_like(igT)
    gate_s[...] = jnp.zeros_like(gate_s)

    @pl.loop(0, joined.shape[1] // TILE)
    def _(t):
        cols = pl.ds(pl.multiple_of(t * TILE, TILE), TILE)
        tokT[cols, :] = joined[:, cols].T

    def zseq(i, parity):
        return 2 * ((z + n_z - 1 - i) % n_z) + parity

    def stage_a(t):
        for i in order:
            mine = W.at[rblk(zseq(i, c)), subq(t, g)]
            arrived(mine, w_r.at[t, i, 0])
            send(mine, mine, w_s.at[t, i, 1], w_r.at[t, i, 1], to_x)
            send(mine, mine, w_s.at[t, i, 2], w_r.at[t, i, 2], to_y)

    def stage_b(t):
        for i in order:
            sq = zseq(i, c)
            ref = W.at[rblk(sq), subq(t, gx)]
            arrived(ref, w_r.at[t, i, 1])
            h = W.at[rhalf(sq, 0), subq(t, gx)]
            send(h, h, w_s.at[t, i, 3], w_r.at[t, i, 3], to_y)
            ref = W.at[rblk(sq), subq(t, gy)]
            arrived(ref, w_r.at[t, i, 2])
            h = W.at[rhalf(sq, 1), subq(t, gy)]
            send(h, h, w_s.at[t, i, 4], w_r.at[t, i, 4], to_x)

    def stage_c(t):
        for i in order:
            sq = zseq(i, c)
            arrived(W.at[rhalf(sq, 0), subq(t, gd)], w_r.at[t, i, 3])
            arrived(W.at[rhalf(sq, 1), subq(t, gd)], w_r.at[t, i, 4])
            ref = W.at[rblk(sq), tile(t)]
            send(ref, ref, wp_s.at[t, i], wp_r.at[t, i], partner)

    def stage_d(t):
        arrived(W.at[rblk(2 * z + 1 - c), tile(t)], wp_r.at[t, n_z - 1])
        for i in order:
            arrived(W.at[rblk(zseq(i, 1 - c)), tile(t)], wp_r.at[t, i])

    def lanes(v):
        out = v[:, 0:128]
        for q in range(1, TILE // 128):
            out = out + v[:, 128 * q : 128 * q + 128]
        return out

    def forward(t):
        cols = tile(t)
        pre_s[...] = jnp.dot(joined[...], W[:, cols], preferred_element_type=f32)

        def common(ch):
            sv = score_ref[:, cols]
            pre = pre_s[ch, :]
            sig = 1.0 / (1.0 + jnp.exp(-pre))
            gate_s[ch, :] += lanes(pre * sig * sv)
            sl = sig * (1.0 + pre * (1.0 - sig)) * sv
            slope_s[ch, cols] = sl
            return sv, pre, sig, sl

        @pl.loop(0, toks // CHUNK)
        def _(u):
            common(pl.ds(pl.multiple_of(u * CHUNK, CHUNK), CHUNK))

        @pl.loop(0, toks // CHUNK)
        def _(u):
            ch = pl.ds(pl.multiple_of(u * CHUNK, CHUNK), CHUNK)
            sv, pre, sig, sl = common(pl.ds(pl.multiple_of(toks + u * CHUNK, CHUNK), CHUNK))
            R[2, ch, cols] = sl.astype(bf16)
            curve_s[ch, cols] = sig * (1.0 - sig) * (2.0 + pre * (1.0 - 2.0 * sig)) * sv

        send(R.at[2, :, cols], RP.at[2, :, cols], R_s.at[2, t], R_r.at[2, t], partner)
        liftT[...] = R[2, :, cols].T

        @pl.loop(0, W.shape[0] // TILE)
        def _(u):
            ch = pl.ds(pl.multiple_of(u * TILE, TILE), TILE)
            igT[ch, :] += jnp.dot(W[ch, cols], liftT[...], preferred_element_type=f32)

    stage_a(0)
    for b in range(n_z):
        send(tokT.at[rblk(2 * b + 1 - c), :], tokP.at[b], tok_s.at[b], tok_r.at[b], partner, True)
    stage_b(0)

    @pl.loop(0, n_tiles)
    def _(t):
        @pl.when(t + 1 < n_tiles)
        def _():
            stage_a(t + 1)

        stage_c(t)
        stage_d(t)
        forward(t)

        @pl.when(t + 1 < n_tiles)
        def _():
            stage_b(t + 1)

    @pl.loop(0, W.shape[0] // TILE)
    def _(t):
        cols = pl.ds(pl.multiple_of(t * TILE, TILE), TILE)
        r = (loss_scale * R1_WEIGHT * igT[cols, :]).astype(bf16)
        r1T[cols, :] = r
        r1[:, cols] = r.T

    for b in range(n_z):
        send(r1T.at[rblk(2 * b + 1 - c), :], r1P.at[b], r1_s.at[b], r1_r.at[b], partner, True)

    gate = jnp.sum(gate_s[...], axis=1, keepdims=True)
    gate_s[0:toks, :] = jnp.broadcast_to(loss_scale / (1.0 + jnp.exp(-gate[:toks])), (toks, 128))
    gate_s[toks : 2 * toks, :] = jnp.broadcast_to(-loss_scale / (1.0 + jnp.exp(gate[toks:])), (toks, 128))

    def gated(ch, cols):
        return jnp.concatenate([gate_s[ch, :]] * (TILE // 128), 1) * slope_s[ch, cols]

    @pl.loop(0, n_tiles)
    def _(t):
        cols = tile(t)
        pre_s[0:toks, :] = jnp.dot(r1[...], W[:, cols], preferred_element_type=f32)

        @pl.loop(0, toks // CHUNK)
        def _(u):
            ch = pl.ds(pl.multiple_of(u * CHUNK, CHUNK), CHUNK)
            R[0, ch, cols] = gated(ch, cols).astype(bf16)
            low = pl.ds(pl.multiple_of(toks + u * CHUNK, CHUNK), CHUNK)
            R[1, ch, cols] = (gated(low, cols) + pre_s[ch, :] * curve_s[ch, cols]).astype(bf16)

        send(R.at[0:2, :, cols], RP.at[0:2, :, cols], R_s.at[0, t], R_r.at[0, t], partner)

    for b in range(n_z):
        arrived(tokP.at[b], tok_r.at[b])
        arrived(r1P.at[b], r1_r.at[b])
    @pl.loop(0, n_tiles)
    def _(t):
        arrived(RP.at[2, :, tile(t)], R_r.at[2, t])
        arrived(RP.at[0:2, :, tile(t)], R_r.at[0, t])

    last = n_z - 1

    def hop(k):
        return (z + 1 + k) % n_z

    def block(k, own=False):
        zb = hop(k)
        mine = rblk(2 * zb + c)

        @pl.loop(0, n_tiles)
        def _(t):
            cols = pl.ds(pl.multiple_of(t * TILE, TILE), TILE)
            acc = jnp.dot(tokT[mine, :], R[0:2, :, cols].reshape(2 * toks, TILE), preferred_element_type=f32)
            acc += jnp.dot(r1T[mine, :], R[2, :, cols], preferred_element_type=f32)
            acc += jnp.dot(tokP[zb], RP[0:2, :, cols].reshape(2 * toks, TILE), preferred_element_type=f32)
            acc += jnp.dot(r1P[zb], RP[2, :, cols], preferred_element_type=f32)
            G[k, :, cols] = acc

    def over(m, body):
        @pl.loop(0, m // CHUNK)
        def _(u):
            body(pl.multiple_of(u * CHUNK, CHUNK))

    def at(start):
        return pl.ds(pl.multiple_of(start, CHUNK), CHUNK)

    def spans(own):
        if not own:
            return 0, xr + zrow, xr
        return 0, hr, hr

    def step1(k, own=False):
        bx, by, m = spans(own)
        for j in range(2):
            def put_x(r):
                ex1[k, j, at(r), :] = encode(G[k, at(bx + r), quarter(2 * j + 1 - x)])

            over(m, put_x)
            part = pl.ds(0, m)
            send(ex1.at[k, j, part], rx1.at[k, j, part], g_s.at[k, j], g_r.at[k, j], to_x)

            def put_y(r):
                ey1[k, j, at(r), :] = encode(G[k, at(by + r), quarter(2 * (1 - y) + j)])

            over(m, put_y)
            send(ey1.at[k, j, part], ry1.at[k, j, part], g_s.at[k, 2 + j], g_r.at[k, 2 + j], to_y)

    def step2(k, own=False):
        bx, by, m = spans(own)
        part = pl.ds(0, m)
        for j in range(2):
            arrived(rx1.at[k, j, part], g_r.at[k, j])
            arrived(ry1.at[k, j, part], g_r.at[k, 2 + j])

        def put_x(r):
            ex2[k, at(r), :] = encode(G[k, at(bx + r), quarter(gy)] + decode(rx1[k, 1 - y, at(r), :]))

        over(m, put_x)
        send(ex2.at[k, part], rx2.at[k, part], g_s.at[k, 4], g_r.at[k, 4], to_y)

        def put_y(r):
            ey2[k, at(r), :] = encode(G[k, at(by + r), quarter(gx)] + decode(ry1[k, 1 - x, at(r), :]))

        over(m, put_y)
        send(ey2.at[k, part], ry2.at[k, part], g_s.at[k, 5], g_r.at[k, 5], to_x)

    def step3(k, own=False):
        bx, by, m = spans(own)
        arrived(rx2.at[k, pl.ds(0, m)], g_r.at[k, 4])
        arrived(ry2.at[k, pl.ds(0, m)], g_r.at[k, 5])

        def sum_x(r):
            return G[k, at(bx + r), quarter(g)] + decode(rx1[k, y, at(r), :]) + decode(rx2[k, at(r), :])

        def sum_y(r):
            return G[k, at(by + r), quarter(g)] + decode(ry1[k, x, at(r), :]) + decode(ry2[k, at(r), :])

        if not own:
            def put(r):
                S[k, at(r), :] = encode(sum_x(r))
                S[k, at(xr + r), :] = encode(sum_y(r))

            over(m, put)
            send(S.at[k], rz.at[k], z_s.at[k], z_r.at[k], to_z(hop(k)))
        else:
            def far(r):
                out = decode(rz[0, at(r), :])
                for i in range(1, last):
                    out = out + decode(rz[i, at(r), :])
                return out

            def both(r):
                A[g, at(r), :] = encode(sum_x(r) + far(r))
                A[g, at(xr + zrow + r), :] = encode(sum_y(xr + zrow - hr + r) + far(xr + r))

            over(xr, both)

    def unpack(j):
        def put(r):
            out_ref[at(r), quarter(j)] = decode(A[j, at(r), :])

        over(rows, put)

    @pl.loop(0, last)
    def _(k):
        block(k)
        step1(k)

        @pl.when(k >= 1)
        def _():
            step2(k - 1)

    block(last, True)
    step1(last, True)

    @pl.loop(0, last)
    def _(k):
        @pl.when(k == 1)
        def _():
            step2(last - 1)

        step3(k)

    step2(last, True)
    for k in range(last):
        arrived(rz.at[k], z_r.at[k])
    step3(last, True)
    send(A.at[g], A.at[g], a_s.at[0], a_r.at[0], to_x, True)
    send(A.at[g], A.at[g], a_s.at[1], a_r.at[1], to_y, True)
    unpack(g)
    lo, hi = pl.ds(0, hr), pl.ds(hr, hr)
    arrived(A.at[gx], a_r.at[0])
    send(A.at[gx, lo], A.at[gx, lo], a_s.at[2], a_r.at[2], to_y, True)
    arrived(A.at[gy], a_r.at[1])
    send(A.at[gy, hi], A.at[gy, hi], a_s.at[3], a_r.at[3], to_x, True)
    unpack(gx)
    unpack(gy)
    arrived(A.at[gd, lo], a_r.at[2])
    arrived(A.at[gd, hi], a_r.at[3])
    unpack(gd)
    for cp in pending:
        cp.wait_send()

    @pl.loop(0, n_tiles)
    def _(t):
        for i in order:
            for m in range(3):
                sent(W.at[0:rows, 0:sub], w_s.at[t, i, m])
            for m in range(3, 5):
                sent(W.at[0:hr, 0:sub], w_s.at[t, i, m])
        for i in range(n_z):
            sent(W.at[0:rows, 0:TILE], wp_s.at[t, i])
        sent(R.at[2, :, tile(t)], R_s.at[2, t])
        sent(R.at[0:2, :, tile(t)], R_s.at[0, t])

    def drain(k, own=False):
        part = pl.ds(0, spans(own)[2])
        for j in range(2):
            sent(ex1.at[k, j, part], g_s.at[k, j])
            sent(ey1.at[k, j, part], g_s.at[k, 2 + j])
        sent(ex2.at[k, part], g_s.at[k, 4])
        sent(ey2.at[k, part], g_s.at[k, 5])
        if not own:
            sent(S.at[k], z_s.at[k])

    @pl.loop(0, last)
    def _(k):
        drain(k)

    drain(last, True)


def fused(n_z, loss_scale, fake_tokens, real_tokens, proj_weight, score_vector):
    toks, d_in = fake_tokens.shape[1:]
    rows, hid = proj_weight.shape
    f32, bf16 = jnp.float32, jnp.bfloat16
    vm, dma = pltpu.VMEM, pltpu.SemaphoreType.DMA
    tiles = hid // TILE
    hr = rows // 2
    xr = hr
    scratch = [
        vm((d_in, hid), bf16),
        vm((2 * toks, d_in), bf16),
        vm((d_in, 2 * toks), bf16),
        vm((n_z, rows, 2 * toks), bf16),
        vm((d_in, toks), f32),
        vm((TILE, toks), bf16),
        vm((toks, d_in), bf16),
        vm((d_in, toks), bf16),
        vm((n_z, rows, toks), bf16),
        vm((3, toks, hid), bf16),
        vm((3, toks, hid), bf16),
        vm((2 * toks, TILE), f32),
        vm((2 * toks, hid), f32),
        vm((toks, hid), f32),
        vm((2 * toks, 128), f32),
        vm((n_z, rows, hid), f32),
        vm((n_z, 2, hr, CODED), bf16),
        vm((n_z, 2, hr, CODED), bf16),
        vm((n_z, hr, CODED), bf16),
        vm((n_z, hr, CODED), bf16),
        vm((n_z, 2, hr, CODED), bf16),
        vm((n_z, 2, hr, CODED), bf16),
        vm((n_z, hr, CODED), bf16),
        vm((n_z, hr, CODED), bf16),
        vm((n_z - 1, 2 * xr, CODED), bf16),
        vm((n_z - 1, 2 * xr, CODED), bf16),
        vm((4, rows, CODED), bf16),
        dma((tiles, n_z - 1, 5)), dma((tiles, n_z - 1, 5)),
        dma((tiles, n_z)), dma((tiles, n_z)),
        dma((n_z,)), dma((n_z,)),
        dma((n_z,)), dma((n_z,)),
        dma((3, tiles)), dma((3, tiles)),
        dma((n_z, 6)), dma((n_z, 6)),
        dma((n_z - 1,)), dma((n_z - 1,)),
        dma((4,)), dma((4,)),
    ]
    return pl.pallas_call(
        functools.partial(kernel, n_z, loss_scale),
        out_shape=jax.ShapeDtypeStruct((rows, hid), f32),
        in_specs=[pl.BlockSpec(memory_space=pltpu.VMEM)] * 4,
        out_specs=pl.BlockSpec(memory_space=pltpu.VMEM),
        scratch_shapes=scratch,
        compiler_params=pltpu.CompilerParams(
            collective_id=0, has_side_effects=True, vmem_limit_bytes=58 * 1024 * 1024
        ),
    )(fake_tokens[0], real_tokens[0], proj_weight, score_vector[None, :])


def solution(mesh):
    in_specs = (P("grp", "seq", None), P("grp", "seq", None), P("seq", None), P())
    out_specs = P("seq", None)
    n_grp, n_seq = mesh.shape["grp"], mesh.shape["seq"]

    def body(fake_tokens, real_tokens, proj_weight, score_vector):
        toks = fake_tokens.shape[1]
        rows, hid = proj_weight.shape
        fits = n_grp == 4 and n_seq == 8 and hid == 4 * TILE and rows % 192 == 0 and toks % 64 == 0
        if not fits:
            return per_device(fake_tokens, real_tokens, proj_weight, score_vector)
        loss_scale = math.sqrt(hid / (n_grp * n_seq * toks))
        return fused(n_seq // 2, loss_scale, fake_tokens, real_tokens, proj_weight, score_vector)

    return jax.shard_map(body, mesh=mesh, in_specs=in_specs, out_specs=out_specs, check_vma=False)
```
